512 devices in a mesh: tm: 64 (over y, z_hi, core), height: 8 (over x, z_lo).
Axes of the slice: x: 4, y: 8, z: 8 (z_hi: 4, z_lo: 2; z = z_hi * 2 + z_lo), core: 2. Of those that a mesh axis runs over, the one named last changes fastest.
Arguments:
- coarse_input: bfloat16 [192, 32, 16, 512], P('tm', 'height'), may hold values from -450 to 450
- cotangent: bfloat16 [192, 64, 32, 256], P('tm', 'height'), may hold values from -45 to 45
- conv_kernel: bfloat16 [27, 512, 256], P(None, None, 'tm'), may hold values from -0.0546875 to 0.0546875
- short_kernel: bfloat16 [1, 512, 256], P(None, None, 'tm'), may hold values from -0.25 to 0.25
- norm_gain: float32 [512], replicated, may hold values from 0.5 to 2
- norm_bias: float32 [512], replicated, may hold values from -3 to 3
- frame_lengths: int32 [64], replicated, may hold values from 1 to 3, 97 in all
- row_lengths: int32 [8], replicated, may hold values from 1 to 4, 17 in all
Outputs:
- coarse_grad: float32 [192, 32, 16, 512], P('tm', 'height')
The draws below stay inside these ranges and needn't reach their ends.
Inputs may be any that keep to these rules, and one draw needn't show every extreme that they name: `frame_lengths`: the entries sum to 97, and some tm index holds 3 frames. `row_lengths`: the entries sum to 17, and some height index holds 4 coarse rows.
All inputs are finite; a program needn't handle non-finite values.
Results may differ from the reference program's by a relative error of at most 0.00035.
Values may be sent and summed in bfloat16 or wider, within the bound.
A program may use at most 128 MiB of HBM per device.

```python
import math
import jax
import jax.numpy as jnp
import numpy as np
from jax import lax

C_MID = 512
C_OUT = 256
GROUPS = 32
F_SLOT = 3
R_SLOT = 4
WC = 16
FRAMES = 97
ROWS = 17
SLOT_FRAMES = 192
SLOT_ROWS = 32
N_TM = 64
N_HEIGHT = 8


def growth(length):
    return jnp.exp(math.log(3.0) * jnp.arange(length, dtype=jnp.float32) / (length - 1))


def draw_coarse_input(key, part):
    key = jax.random.fold_in(key, 11)
    key_noise, key_spread, key_chan, key_offset = jax.random.split(key, 4)
    shape = (SLOT_FRAMES, SLOT_ROWS, WC, C_MID)
    noise = jnp.clip(jax.random.normal(key_noise, shape, jnp.float32), -4.0, 4.0)
    spread = jnp.exp(jax.random.uniform(key_spread, (SLOT_FRAMES, SLOT_ROWS, WC, 1), jnp.float32, 0.0, math.log(10.0)))
    channel_scale = jnp.exp(jax.random.uniform(key_chan, (C_MID,), jnp.float32, 0.0, math.log(10.0)))
    offset = jax.random.uniform(key_offset, (C_MID,), jnp.float32, -1.0, 1.0)
    scale = growth(SLOT_FRAMES)[:, None, None, None] * growth(SLOT_ROWS)[None, :, None, None] * spread * channel_scale / 10.0
    return ((offset + noise) * scale).astype(jnp.bfloat16)


def draw_cotangent(key, part):
    key = jax.random.fold_in(key, 12)
    key_noise, key_spread, key_common = jax.random.split(key, 3)
    shape = (SLOT_FRAMES, 2 * SLOT_ROWS, 2 * WC, C_OUT)
    noise = jnp.clip(jax.random.normal(key_noise, shape, jnp.float32), -4.0, 4.0)
    common = 0.5 * jax.random.uniform(key_common, (C_OUT,), jnp.float32, -1.0, 1.0)
    spread = jnp.exp(jax.random.uniform(key_spread, (SLOT_FRAMES, 2 * SLOT_ROWS, 2 * WC, 1), jnp.float32, 0.0, math.log(4.0)))
    scale = growth(SLOT_FRAMES)[:, None, None, None] * growth(2 * SLOT_ROWS)[None, :, None, None] * spread / 4.0
    return ((common + noise) * scale).astype(jnp.bfloat16)


def block_scale(key, extent, pieces, least, largest):
    def one(axis_at, blocks):
        steps = jax.random.uniform(jax.random.fold_in(jax.random.fold_in(key, 6), axis_at), (blocks,), jnp.float32, least / len(pieces), largest / len(pieces))
        return jnp.repeat(jnp.exp(steps), extent[axis_at] // blocks).reshape((-1,) + (1,) * (len(extent) - axis_at - 1))

    gain = one(*pieces[0])
    for cut in pieces[1:]:
        gain = gain * one(*cut)
    return gain


def split_up(count, total, most, skew):
    loads = [(1 << 20) // math.isqrt(grade ** skew) + 1 for grade in range(2, count + 1)]
    spare, given = total - most - (count - 1), [1] * (count - 1)
    while spare > 0:
        candidates = [i for i in range(count - 1) if given[i] < most]
        whole, left = sum([loads[i] for i in candidates]), spare
        for i in candidates:
            addition = min(most - given[i], max(1, left * loads[i] // whole), spare)
            given[i] = given[i] + addition
            spare = spare - addition
    return np.array([most] + given)


def ragged_sizes(rng, count, total, limit, slope):
    if count == 2:
        one = jax.random.randint(rng, (), max(1, total - limit), min(limit, total - 1) + 1)
        return jnp.stack([one, total - one])
    tallies = jnp.asarray(split_up(count, total, limit, slope), jnp.int32)
    pairs = (count - 1) // 2
    source_of, sink = tallies[1:1 + 2 * pairs:2], tallies[2:2 + 2 * pairs:2]
    margin = jnp.minimum(source_of - 1, limit - sink)
    shifted = jax.random.randint(jax.random.fold_in(rng, 1), (pairs,), 0, 1 << 20) % (margin + 1)
    tallies = tallies.at[1:1 + 2 * pairs:2].set(source_of - shifted).at[2:2 + 2 * pairs:2].set(sink + shifted)
    return tallies[jax.random.permutation(jax.random.fold_in(rng, 2), count)]


def gaussian(stream_key, shape, deviation, reach, pieces=(), kind=jnp.bfloat16):
    array = jax.random.normal(stream_key, shape, jnp.float32) * deviation
    if len(pieces) > 0:
        array = block_scale(stream_key, shape, pieces, -0.22, 0.18) * array
    return jnp.clip(array, min=-reach, max=reach).astype(kind)


def setup_inputs(seed: int = 0) -> dict:
    key_list = jax.random.split(jax.random.key(seed), 9)
    coarse_input = draw_coarse_input(jax.random.fold_in(key_list[8], 71), 0)
    cotangent = draw_cotangent(jax.random.fold_in(key_list[8], 71), 0)
    conv_kernel = gaussian(key_list[2], (27, C_MID, C_OUT), (27 * C_MID) ** -0.5, 0.0546875, ((2, 64),))
    short_kernel = gaussian(key_list[3], (1, C_MID, C_OUT), C_MID ** -0.5, 0.25, ((2, 64),))
    norm_gain = jnp.clip(jnp.exp(jax.random.uniform(key_list[4], (C_MID,), jnp.float32, math.log(0.5), math.log(2.0))), 0.5, 2.0)
    norm_bias = gaussian(key_list[5], (C_MID,), 1.0, 3.0, (), jnp.float32)
    frame_lengths = ragged_sizes(key_list[6], N_TM, FRAMES, F_SLOT, 1).astype(jnp.int32)
    row_lengths = ragged_sizes(key_list[7], N_HEIGHT, ROWS, R_SLOT, 0).astype(jnp.int32)
    return dict(coarse_input=coarse_input, cotangent=cotangent, conv_kernel=conv_kernel, short_kernel=short_kernel, norm_gain=norm_gain, norm_bias=norm_bias, frame_lengths=frame_lengths, row_lengths=row_lengths)


EPSILON = 1e-06

def slot_positions(lengths, slots, total):
    owners = jnp.repeat(lengths, slots, total_repeat_length=lengths.shape[0] * slots)
    offsets = jnp.tile(jnp.arange(slots, dtype=jnp.int32), lengths.shape[0])
    return jnp.nonzero(offsets < owners, size=total, fill_value=0)[0].astype(jnp.int32)

def group_totals(values, groups):
    shaped = values.reshape(values.shape[:-1] + (groups, values.shape[-1] // groups))
    return lax.optimization_barrier(jnp.sum(shaped, axis=(0, 1, 2, 4)))

def per_channel(statistics, channels):
    return jnp.repeat(statistics, channels // statistics.shape[0])

def pool_pairs(values):
    frames, rows, columns, channels = values.shape
    return values.reshape(frames, rows // 2, 2, columns // 2, 2, channels).sum(axis=(2, 4))

def reference(coarse_input, cotangent, conv_kernel, short_kernel, norm_gain, norm_bias, frame_lengths, row_lengths):
    frame_slots = slot_positions(frame_lengths, F_SLOT, FRAMES)
    row_slots = slot_positions(row_lengths, R_SLOT, ROWS)
    fine_slots = (2 * row_slots[:, None] + jnp.arange(2, dtype=jnp.int32)[None, :]).reshape(-1)
    video = coarse_input[frame_slots][:, row_slots].astype(jnp.float32)
    fine_cot = cotangent[frame_slots][:, fine_slots].astype(jnp.float32)
    total_count = float(FRAMES * ROWS * WC * (C_MID // GROUPS))
    group_mean = group_totals(video, GROUPS) / total_count
    inverse_std = lax.rsqrt(group_totals(video * video, GROUPS) / total_count - group_mean * group_mean + EPSILON)
    mean_chan = per_channel(group_mean, C_MID)
    inverse_chan = per_channel(inverse_std, C_MID)
    normed = (video - mean_chan) * inverse_chan
    pre_act = normed * norm_gain + norm_bias
    sigmoid_pre = jax.nn.sigmoid(pre_act)
    silu_slope = sigmoid_pre * (1.0 + pre_act * (1.0 - sigmoid_pre))
    kernel = conv_kernel.astype(jnp.float32).reshape(3, 3, 3, C_MID, C_OUT)[::-1, ::-1, ::-1].transpose(0, 1, 2, 4, 3)
    conv_grad = lax.conv_general_dilated(fine_cot[None], kernel, (1, 1, 1), ((0, 2), (1, 1), (1, 1)), dimension_numbers=('NDHWC', 'DHWIO', 'NDHWC'), precision=lax.Precision.HIGHEST)[0]
    skip_grad = jnp.einsum('thwo,io->thwi', fine_cot, short_kernel[0].astype(jnp.float32), precision=lax.Precision.HIGHEST)
    pooled = pool_pairs(conv_grad)
    skip_pooled = pool_pairs(skip_grad)
    grad_hat = pooled * silu_slope * norm_gain
    slope_sum = group_totals(grad_hat, GROUPS)
    slope_cross = group_totals(grad_hat * normed, GROUPS)
    coarse_grad = inverse_chan * (grad_hat - (per_channel(slope_sum, C_MID) + normed * per_channel(slope_cross, C_MID)) / total_count) + skip_pooled
    output = jnp.zeros(coarse_input.shape, jnp.float32)
    return output.at[frame_slots[:, None], row_slots[None, :]].set(coarse_grad)
```

```python
import functools

import jax
import jax.numpy as jnp
from jax import lax
from jax.experimental import pallas as pl
from jax.experimental.pallas import tpu as pltpu
from jax.sharding import PartitionSpec as P

EPSILON = 1e-06
COUNT = 422144.0
TAPS = ((0, 16), (16, 12))
BF = jnp.bfloat16
F32 = jnp.float32


def mod(value, n):
    return lax.rem(value + n, n)


class Table:
    def __init__(self, send, recv):
        self.send, self.recv, self.entries, self.count = send, recv, {}, 0

    def add(self, name, src, dst, device):
        self.entries[name] = (src, dst, device, self.count)
        self.count += 1

    def get(self, name):
        src, dst, device, at = self.entries[name]
        return pltpu.make_async_remote_copy(
            src_ref=src() if callable(src) else src,
            dst_ref=dst() if callable(dst) else dst,
            send_sem=self.send.at[at],
            recv_sem=self.recv.at[at],
            device_id=device,
            device_id_type=pl.DeviceIdType.MESH,
        )

    def start(self, *names):
        for name in names:
            self.get(name).start()

    def arrive(self, *names):
        for name in names:
            self.get(name).wait_recv()

    def sent(self, *names):
        for name in names:
            self.get(name).wait_send()


def kernel(
    fl_ref, rl_ref, y_ref, g_ref, wc_ref, ws_ref, gain_ref, bias_ref, out_ref,
    whole, mine, slots, rows32, ahead, edge_out, edge_in, padded, windows,
    acc, skip, hat, slope, ar, ar_send, ar_recv, small_send, small_recv,
    send0, recv0, send1, recv1,
):
    tm, height = lax.axis_index("tm"), lax.axis_index("height")
    y, h, c = tm // 8, lax.rem(tm // 2, 4), lax.rem(tm, 2)
    x, zl = height // 2, lax.rem(height, 2)
    fl, rl = fl_ref[tm], rl_ref[height]
    fl_next = fl_ref[mod(tm + 1, 64)]

    def at(y_=y, h_=h, c_=c, x_=x, z_=zl):
        return (y_ * 8 + h_ * 2 + c_, x_ * 2 + z_)

    partners = []
    for d in range(1, 8):
        q = lax.rem(h * 2 + c + d, 8)
        partners.append(at(h_=q // 2, c_=lax.rem(q, 2)))
        partners.append(at(y_=lax.rem(y + d, 8)))
    for d in range(1, 4):
        partners.append(at(x_=lax.rem(x + d, 4)))
        partners.append(at(x_=lax.rem(x + d, 4), c_=1 - c))
    for d in range(4):
        partners.append(at(h_=lax.rem(h + d, 4), z_=1 - zl))
    for d in (1, 2, 62, 63):
        partners.append((lax.rem(tm + d, 64), height))
    for d in (1, 7):
        partners.append((tm, lax.rem(height + d, 8)))
    barrier = pltpu.get_barrier_semaphore()
    for partner in partners:
        pl.semaphore_signal(barrier, inc=1, device_id=partner, device_id_type=pl.DeviceIdType.MESH)

    def ar_copy(turn, step, d):
        if step == 0:
            own = x * 2 + c
            other = lax.rem(own + d, 8)
            device = at(x_=other // 2, c_=lax.rem(other, 2))
        elif step == 1:
            own = y
            device = at(y_=lax.rem(own + d, 8))
        else:
            own = h * 2 + zl
            other = lax.rem(own + d, 8)
            device = at(h_=other // 2, z_=lax.rem(other, 2))
        place = ar.at[turn, step, own]
        return own, pltpu.make_async_remote_copy(
            src_ref=place, dst_ref=place,
            send_sem=ar_send.at[turn, step, d - 1], recv_sem=ar_recv.at[turn, step, d - 1],
            device_id=device, device_id_type=pl.DeviceIdType.MESH,
        )

    def ar_begin(turn, step, value):
        own, _ = ar_copy(turn, step, 1)
        ar[turn, step, own] = value
        for d in range(1, 8):
            ar_copy(turn, step, d)[1].start()

    def ar_end(turn, step):
        for d in range(1, 8):
            ar_copy(turn, step, d)[1].wait_recv()
        return jnp.sum(ar[turn, step], axis=0)

    def tile_of(first, second):
        parts = [v[:, 128 * k : 128 * k + 128] for v in (first, second) for k in range(4)]
        return jnp.concatenate(parts, axis=0)

    def row_of(tile, base):
        return jnp.concatenate([tile[base + k : base + k + 1] for k in range(4)], axis=1)

    same = (lax.broadcasted_iota(jnp.int32, (128, 128), 0) >> 4) == (
        lax.broadcasted_iota(jnp.int32, (128, 128), 1) >> 4
    )
    group_ones = jnp.where(same, 1.0, 0.0).astype(F32)

    def group_total(tile):
        return jnp.dot(tile, group_ones, precision=lax.Precision.HIGHEST, preferred_element_type=F32)

    first = jnp.zeros((16, 512), F32)
    second = jnp.zeros((16, 512), F32)
    for f in range(3):
        for r in range(4):
            live = jnp.where((f < fl) & (r < rl), 1.0, 0.0).astype(F32)
            value = y_ref[f, r].astype(F32) * live
            first = first + value
            second = second + value * value
    stats = tile_of(jnp.sum(first, axis=0, keepdims=True), jnp.sum(second, axis=0, keepdims=True))
    mine[0:27] = wc_ref[...]
    mine[27:28] = ws_ref[...]

    def table(role):
        t0, taps = TAPS[role]
        half = taps // 2
        t = Table(send0 if role == 0 else send1, recv0 if role == 0 else recv1)

        def piece(column, block, lo=0, n=taps):
            row = pl.multiple_of(block * 32, 32)
            return whole.at[pl.ds(t0 + lo, n), column, pl.ds(row, 32)]

        for d in range(1, 4):
            device = at(h_=lax.rem(h + d, 4), c_=role)
            lane = pl.multiple_of(x * 128, 128)
            src = mine.at[pl.ds(t0, taps), :, pl.ds(lane, 128)]
            t.add(f"a{d}0", src, slots.at[pl.ds(0, taps), h * 2 + 0], device)
            t.add(f"a{d}1", src, slots.at[pl.ds(0, taps), h * 2 + 1], device)
        t.add("as", src, slots.at[pl.ds(0, taps), h * 2 + 1 - role], at(c_=role))
        columns = [x, mod(x - 1, 4), mod(x + 1, 4), mod(x + 2, 4)]
        blocks = [y]
        for s in range(1, 4):
            blocks += [mod(y - s, 8), mod(y + s, 8)]
        blocks.append(mod(y + 4, 8))
        left, right = at(x_=mod(x - 1, 4)), at(x_=mod(x + 1, 4))
        up, down = at(y_=mod(y + 1, 8)), at(y_=mod(y - 1, 8))
        for k in range(8 if role == 0 else 1):
            b = blocks[k]
            for name, column, lo, n, device in (
                (f"xr{k}", 0, 0, taps, right),
                (f"xl{k}", 0, 0, taps, left),
                (f"or{k}", 1, 0, half, right),
                (f"ol{k}", 2, half, taps - half, left),
            ):
                ref = piece(columns[column], b, lo, n)
                t.add(name, ref, ref, device)
        for j in range(1 if role == 0 else 4):
            for s in range(4):
                ref = piece(columns[j], mod(y - s, 8), 0, half if s == 3 else taps)
                t.add(f"yp{j}{s}", ref, ref, up)
                ref = piece(columns[j], mod(y + s, 8), half if s == 3 else 0, taps - half if s == 3 else taps)
                t.add(f"ym{j}{s}", ref, ref, down)
        for k in range(8):
            for j in range(4):
                ref = piece(columns[j], blocks[k])
                t.add(f"d{k}{j}", ref, ref, at(c_=1 - role))
        return t

    tables = (table(0), table(1))

    def stage_a_send():
        for role in (0, 1):
            @pl.when(c == 0)
            def _():
                for d in range(1, 4):
                    tables[role].start(f"a{d}0")

            @pl.when(c == 1)
            def _():
                for d in range(1, 4):
                    tables[role].start(f"a{d}1")

            @pl.when(c == 1 - role)
            def _():
                tables[role].start("as")

    def stage_a_sent():
        for role in (0, 1):
            @pl.when(c == 0)
            def _():
                for d in range(1, 4):
                    tables[role].sent(f"a{d}0")

            @pl.when(c == 1)
            def _():
                for d in range(1, 4):
                    tables[role].sent(f"a{d}1")

            @pl.when(c == 1 - role)
            def _():
                tables[role].sent("as")

    def stage_a_arrive(role):
        t0, taps = TAPS[role]
        t = tables[role]
        lane = pl.multiple_of(x * 128, 128)
        slots[0:taps, h * 2 + role] = mine[t0 : t0 + taps, :, pl.ds(lane, 128)]
        for d in range(1, 4):
            t.arrive(f"a{d}0", f"a{d}1")
        t.arrive("as")
        for s in range(8):
            rows32[0:taps, 4 * s : 4 * s + 4] = slots[0:taps, s].astype(F32)
        row = pl.multiple_of(y * 32, 32)
        whole[t0 : t0 + taps, x, pl.ds(row, 32)] = rows32[0:taps].astype(BF)

    def x_in0(k):
        t = tables[0]
        t.arrive(f"xr{k}")
        t.start(f"or{k}", f"d{k}1")
        t.arrive(f"xl{k}")
        t.start(f"ol{k}", f"d{k}2")

    def o_in0(k):
        t = tables[0]
        t.arrive(f"or{k}", f"ol{k}")
        t.start(f"d{k}3")

    def y_in0(s):
        t = tables[0]
        if s < 4:
            k = 2 * s - 1
            t.arrive(f"yp0{s - 1}")
            t.start(f"yp0{s}", f"xr{k}", f"xl{k}", f"d{k}0")
            t.arrive(f"ym0{s - 1}")
            t.start(f"ym0{s}", f"xr{k + 1}", f"xl{k + 1}", f"d{k + 1}0")
        else:
            t.arrive("yp03", "ym03")
            t.start("xr7", "xl7", "d70")

    def x_in1():
        t = tables[1]
        t.arrive("xr0")
        t.start("or0", "yp10", "ym10", "d01")
        t.arrive("xl0")
        t.start("ol0", "yp20", "ym20", "d02")
        t.arrive("or0", "ol0")
        t.start("yp30", "ym30", "d03")

    def y_in1(s):
        t = tables[1]
        for j in range(4):
            if s < 4:
                t.arrive(f"yp{j}{s - 1}")
                t.start(f"yp{j}{s}", f"d{2 * s - 1}{j}")
                t.arrive(f"ym{j}{s - 1}")
                t.start(f"ym{j}{s}", f"d{2 * s}{j}")
            else:
                t.arrive(f"yp{j}3", f"ym{j}3")
                t.start(f"d7{j}")

    def small_copy(which):
        if which == 0:
            src, dst, device = g_ref.at[pl.ds(0, 2)], ahead.at[pl.ds(0, 2)], (mod(tm - 1, 64), height)
        elif which == 1:
            src, dst, device = g_ref.at[0], ahead.at[2], (lax.rem(tm + 62, 64), height)
        elif which == 2:
            src, dst, device = edge_out.at[1], edge_in.at[0], (tm, mod(height + 1, 8))
        else:
            src, dst, device = edge_out.at[0], edge_in.at[1], (tm, mod(height - 1, 8))
        return pltpu.make_async_remote_copy(
            src_ref=src, dst_ref=dst, send_sem=small_send.at[which], recv_sem=small_recv.at[which],
            device_id=device, device_id_type=pl.DeviceIdType.MESH,
        )

    zero_frame = jnp.zeros((8, 32, 256), BF)
    zero_row = jnp.zeros((32, 256), BF)

    def order_frames():
        small_copy(0).wait_recv()
        small_copy(1).wait_recv()
        has_one = tm < 63
        has_two = jnp.logical_and(has_one, jnp.logical_or(fl_next >= 2, tm < 62))
        following = lax.select(has_one, ahead[0], zero_frame)
        after = lax.select(fl_next >= 2, ahead[1], ahead[2])
        after = lax.select(has_two, after, zero_frame)
        own = [g_ref[0], g_ref[1], g_ref[2]]
        ordered = [
            own[0],
            lax.select(fl >= 2, own[1], following),
            lax.select(fl >= 3, own[2], lax.select(fl == 2, following, after)),
            lax.select(fl >= 3, following, lax.select(fl == 2, after, zero_frame)),
            lax.select(fl >= 3, after, zero_frame),
        ]
        for p in range(5):
            last = ordered[p][1]
            for r in range(8):
                row = ordered[p][r]
                if r >= 2:
                    row = lax.select(r < 2 * rl, row, zero_row)
                if r >= 3 and r % 2 == 1:
                    last = lax.select(r == 2 * rl - 1, row, last)
                padded[p, r + 1] = row
            edge_out[0, p] = ordered[p][0]
            edge_out[1, p] = last
        small_copy(2).start()
        small_copy(3).start()

    def finish_rows():
        small_copy(2).wait_recv()
        small_copy(3).wait_recv()
        for p in range(5):
            above = lax.select(height > 0, edge_in[0, p], zero_row)
            below = lax.select(height < 7, edge_in[1, p], zero_row)
            padded[p, 0] = above
            for r in (2, 4, 6):
                padded[p, r + 1] = lax.select(r == 2 * rl, below, padded[p, r + 1])
            padded[p, 9] = lax.select(rl == 4, below, zero_row)

    def make_windows():
        out_row = lax.broadcasted_iota(jnp.int32, (64, 320), 0)
        in_row = lax.broadcasted_iota(jnp.int32, (64, 320), 1)
        down_by = (in_row >> 5) - 2 * (out_row >> 4)
        along_by = (in_row & 31) - 2 * (out_row & 15)
        choose = []
        for kh in range(3):
            for kw in range(3):
                dr, dc = down_by - (2 - kh), along_by - (1 - kw)
                hit = ((dr == 0) | (dr == 1)) & ((dc == 0) | (dc == 1))
                choose.append(jnp.where(hit, 1.0, 0.0).astype(F32))
        chosen = jnp.concatenate(choose, axis=0).astype(BF)

        def one(f, carry):
            total = jnp.dot(chosen, padded[f].reshape(320, 256), preferred_element_type=F32)
            top = total.astype(BF)
            rest = (total - top.astype(F32)).astype(BF)
            windows[f, 0] = top.reshape(9, 64, 256)
            windows[f, 1] = rest.reshape(9, 64, 256)
            return carry

        lax.fori_loop(0, 5, one, 0)

    def make_slope(total):
        gs = group_total(total) * (1.0 / COUNT)
        mean, msq = gs[0:4], gs[4:8]
        rstd = lax.rsqrt(msq - mean * mean + EPSILON)
        mean_row, rstd_row = row_of(mean, 0), row_of(rstd, 0)
        gain, bias = gain_ref[...], bias_ref[...]

        def one(i, carry):
            value = (y_ref[i // 4, lax.rem(i, 4)].astype(F32) - mean_row) * rstd_row
            pre = value * gain + bias
            sig = jax.nn.sigmoid(pre)
            hat[i] = value
            slope[i] = sig * (1.0 + pre * (1.0 - sig)) * gain
            return carry

        lax.fori_loop(0, 12, one, 0)
        return rstd_row

    pl.semaphore_wait(barrier, len(partners))
    stage_a_send()
    ar_begin(0, 0, stats)
    small_copy(0).start()
    small_copy(1).start()

    @pl.when(c == 0)
    def _():
        stage_a_arrive(0)
        tables[0].start("yp00", "ym00", "xr0", "xl0", "d00")

    @pl.when(c == 1)
    def _():
        stage_a_arrive(1)
        tables[1].start("xr0", "xl0", "yp00", "ym00", "d00")

    ar_begin(0, 1, ar_end(0, 0))

    @pl.when(c == 0)
    def _():
        y_in0(1)
        x_in0(0)

    @pl.when(c == 1)
    def _():
        x_in1()

    ar_begin(0, 2, ar_end(0, 1))
    order_frames()

    @pl.when(c == 0)
    def _():
        y_in0(2)
        x_in0(1)
        o_in0(0)
        x_in0(2)

    @pl.when(c == 1)
    def _():
        y_in1(1)

    finish_rows()
    make_windows()

    @pl.when(c == 0)
    def _():
        y_in0(3)
        o_in0(1)
        x_in0(3)
        o_in0(2)
        x_in0(4)

    @pl.when(c == 1)
    def _():
        y_in1(2)

    rstd_row = make_slope(ar_end(0, 2))

    @pl.when(c == 0)
    def _():
        y_in0(4)
        o_in0(3)
        x_in0(5)
        o_in0(4)
        x_in0(6)
        o_in0(5)
        x_in0(7)
        o_in0(6)
        o_in0(7)
        for k in range(8):
            tables[1].arrive(*[f"d{k}{j}" for j in range(4)])

    @pl.when(c == 1)
    def _():
        y_in1(3)
        y_in1(4)
        for k in range(8):
            tables[0].arrive(*[f"d{k}{j}" for j in range(4)])

    def kernel_rows(first_tap, n):
        block = whole[pl.ds(first_tap, n)]
        return jnp.concatenate([block[:, k].reshape(n * 256, 128) for k in range(4)], axis=1)

    skip[...] = jnp.dot(
        windows[0:3, :, 4].reshape(384, 256), kernel_rows(27, 1), preferred_element_type=F32
    ).reshape(3, 2, 64, 512)
    acc[...] = jnp.zeros_like(acc)

    def taps_of(i, carry):
        kt, kh = i // 3, lax.rem(i, 3)
        lhs = jnp.concatenate(
            [windows[pl.ds(2 - kt, 3), :, kh * 3 + kw].reshape(384, 256) for kw in range(3)], axis=1
        )
        acc[...] += jnp.dot(lhs, kernel_rows(3 * i, 3), preferred_element_type=F32).reshape(3, 2, 64, 512)
        return carry

    lax.fori_loop(0, 9, taps_of, 0)

    one_sum = jnp.zeros((16, 512), F32)
    two_sum = jnp.zeros((16, 512), F32)
    for f in range(3):
        for r in range(4):
            here = slice(16 * r, 16 * r + 16)
            live = jnp.where((f < fl) & (r < rl), 1.0, 0.0).astype(F32)
            grad = (acc[f, 0, here] + acc[f, 1, here]) * slope[4 * f + r]
            slope[4 * f + r] = grad
            one_sum = one_sum + grad * live
            two_sum = two_sum + grad * hat[4 * f + r] * live
    sums = tile_of(jnp.sum(one_sum, axis=0, keepdims=True), jnp.sum(two_sum, axis=0, keepdims=True))
    ar_begin(1, 0, sums)
    ar_begin(1, 1, ar_end(1, 0))
    ar_begin(1, 2, ar_end(1, 1))
    both = group_total(ar_end(1, 2)) * (1.0 / COUNT)
    b_one, b_two = row_of(both, 0), row_of(both, 4)
    for f in range(3):
        for r in range(4):
            here = slice(16 * r, 16 * r + 16)
            live = jnp.where((f < fl) & (r < rl), 1.0, 0.0).astype(F32)
            value = rstd_row * (slope[4 * f + r] - (b_one + hat[4 * f + r] * b_two))
            out_ref[f, r] = (value + (skip[f, 0, here] + skip[f, 1, here])) * live

    stage_a_sent()
    for which in range(4):
        small_copy(which).wait_send()
    for turn in range(2):
        for step in range(3):
            for d in range(1, 8):
                ar_copy(turn, step, d)[1].wait_send()
    for role in (0, 1):
        @pl.when(c == role)
        def _():
            tables[role].sent(*[n for n in tables[role].entries if n[0] != "a"])


def shards(coarse_input, cotangent, conv_kernel, short_kernel, norm_gain, norm_bias, frame_lengths, row_lengths):
    vmem = pl.BlockSpec(memory_space=pltpu.VMEM)
    smem = pl.BlockSpec(memory_space=pltpu.SMEM)
    copies = (7 + 32 + 8 + 32, 7 + 4 + 32 + 32)
    return pl.pallas_call(
        kernel,
        out_shape=jax.ShapeDtypeStruct((3, 4, 16, 512), F32),
        in_specs=[smem, smem] + [vmem] * 6,
        out_specs=vmem,
        scratch_shapes=[
            pltpu.VMEM((28, 4, 256, 128), BF),
            pltpu.VMEM((28, 4, 512), BF),
            pltpu.VMEM((16, 8, 4, 128), BF),
            pltpu.VMEM((16, 32, 128), F32),
            pltpu.VMEM((3, 8, 32, 256), BF),
            pltpu.VMEM((2, 5, 32, 256), BF),
            pltpu.VMEM((2, 5, 32, 256), BF),
            pltpu.VMEM((5, 10, 32, 256), BF),
            pltpu.VMEM((5, 2, 9, 64, 256), BF),
            pltpu.VMEM((3, 2, 64, 512), F32),
            pltpu.VMEM((3, 2, 64, 512), F32),
            pltpu.VMEM((12, 16, 512), F32),
            pltpu.VMEM((12, 16, 512), F32),
            pltpu.VMEM((2, 3, 8, 8, 128), F32),
            pltpu.SemaphoreType.DMA((2, 3, 7)),
            pltpu.SemaphoreType.DMA((2, 3, 7)),
            pltpu.SemaphoreType.DMA((4,)),
            pltpu.SemaphoreType.DMA((4,)),
            pltpu.SemaphoreType.DMA((copies[0],)),
            pltpu.SemaphoreType.DMA((copies[0],)),
            pltpu.SemaphoreType.DMA((copies[1],)),
            pltpu.SemaphoreType.DMA((copies[1],)),
        ],
        compiler_params=pltpu.CompilerParams(
            collective_id=0, has_side_effects=True, vmem_limit_bytes=40 * 1024 * 1024
        ),
    )(
        frame_lengths, row_lengths, coarse_input, cotangent,
        conv_kernel.transpose(0, 2, 1), short_kernel.transpose(0, 2, 1),
        norm_gain.reshape(1, 512), norm_bias.reshape(1, 512),
    )


def solution(mesh):
    return jax.shard_map(
        shards,
        mesh=mesh,
        in_specs=(
            P("tm", "height", None, None),
            P("tm", "height", None, None),
            P(None, None, "tm"),
            P(None, None, "tm"),
            P(),
            P(),
            P(),
            P(),
        ),
        out_specs=P("tm", "height", None, None),
        check_vma=False,
    )
```

```python
import functools

import jax
import jax.numpy as jnp
from jax import lax
from jax.experimental import pallas as pl
from jax.experimental.pallas import tpu as pltpu
from jax.sharding import PartitionSpec as P

EPSILON = 1e-06
COUNT = 422144.0
TAPS = ((0, 18), (18, 10))
BF = jnp.bfloat16
F32 = jnp.float32


def mod(value, n):
    return lax.rem(value + n, n)


class Table:
    def __init__(self, send, recv):
        self.send, self.recv, self.entries, self.count = send, recv, {}, 0

    def add(self, name, src, dst, device):
        self.entries[name] = (src, dst, device, self.count)
        self.count += 1

    def get(self, name):
        src, dst, device, at = self.entries[name]
        return pltpu.make_async_remote_copy(
            src_ref=src() if callable(src) else src,
            dst_ref=dst() if callable(dst) else dst,
            send_sem=self.send.at[at],
            recv_sem=self.recv.at[at],
            device_id=device,
            device_id_type=pl.DeviceIdType.MESH,
        )

    def start(self, *names):
        for name in names:
            self.get(name).start()

    def arrive(self, *names):
        for name in names:
            self.get(name).wait_recv()

    def sent(self, *names):
        for name in names:
            self.get(name).wait_send()


def ring_distance(d, n):
    return min(d, n - d)


PLANE = sorted(
    [(dx, dy) for dx in range(4) for dy in range(8) if dx + dy],
    key=lambda d: -(ring_distance(d[0], 4) + ring_distance(d[1], 8)),
)
COLUMN = sorted(
    [(dz, dc) for dz in range(8) for dc in range(2) if dz + dc],
    key=lambda d: -(ring_distance(d[0], 8) + d[1]),
)


def kernel(
    fl_any, rl_any, y_any, g_any, wc_any, ws_any, gain_any, bias_any, out_ref,
    fl_ref, rl_ref, y_ref, g_ref, gain_ref, bias_ref, load_sem,
    whole, mine, slots, rows32, ahead, chosen_next, edge_out, edge_in, padded, windows,
    acc, skip, hat, slope, plane, column, plane_send, plane_recv, column_send, column_recv,
    small_send, small_recv, send0, recv0, send1, recv1,
):
    tm, height = lax.axis_index("tm"), lax.axis_index("height")
    y, h, c = tm // 8, lax.rem(tm // 2, 4), lax.rem(tm, 2)
    x, zl = height // 2, lax.rem(height, 2)
    z = h * 2 + zl

    def at(y_=y, z_=z, c_=c, x_=x):
        return (y_ * 8 + (z_ // 2) * 2 + c_, x_ * 2 + lax.rem(z_, 2))

    def plane_device(d):
        return at(x_=lax.rem(x + d[0], 4), y_=lax.rem(y + d[1], 8))

    def column_device(d):
        return at(z_=lax.rem(z + d[0], 8), c_=lax.rem(c + d[1], 2))

    partners = [plane_device(d) for d in PLANE] + [column_device(d) for d in COLUMN]
    for d in (1, 2, 62, 63):
        partners.append((lax.rem(tm + d, 64), height))
    for d in (1, 7):
        partners.append((tm, lax.rem(height + d, 8)))
    barrier = pltpu.get_barrier_semaphore()
    for partner in partners:
        pl.semaphore_signal(barrier, inc=1, device_id=partner, device_id_type=pl.DeviceIdType.MESH)
    loads = [
        pltpu.make_async_copy(src, dst, load_sem.at[k])
        for k, (src, dst) in enumerate((
            (fl_any, fl_ref), (rl_any, rl_ref), (y_any, y_ref), (wc_any, mine.at[pl.ds(0, 27)]),
            (ws_any, mine.at[pl.ds(27, 1)]), (g_any, g_ref), (gain_any, gain_ref), (bias_any, bias_ref),
        ))
    ]
    for load in loads:
        load.start()
    loads[0].wait()
    loads[1].wait()
    fl, rl = fl_ref[tm], rl_ref[height]
    fl_next = fl_ref[mod(tm + 1, 64)]

    def ar_copy(turn, step, k):
        if step == 0:
            place, device = plane.at[turn, x * 8 + y], plane_device(PLANE[k])
            sems = plane_send.at[turn, k], plane_recv.at[turn, k]
        else:
            place, device = column.at[turn, z * 2 + c], column_device(COLUMN[k])
            sems = column_send.at[turn, k], column_recv.at[turn, k]
        return pltpu.make_async_remote_copy(
            src_ref=place, dst_ref=place, send_sem=sems[0], recv_sem=sems[1],
            device_id=device, device_id_type=pl.DeviceIdType.MESH,
        )

    def ar_begin(turn, step, value):
        if step == 0:
            plane[turn, x * 8 + y] = value
        else:
            column[turn, z * 2 + c] = value
        for k in range((31, 15)[step]):
            ar_copy(turn, step, k).start()

    def ar_end(turn, step):
        for k in range((31, 15)[step]):
            ar_copy(turn, step, k).wait_recv()
        return jnp.sum((plane, column)[step][turn], axis=0)

    def row_of(tile, base):
        return jnp.concatenate([tile[base + k : base + k + 1] for k in range(4)], axis=1)

    lane_i = lax.broadcasted_iota(jnp.int32, (128, 128), 0)
    lane_j = lax.broadcasted_iota(jnp.int32, (128, 128), 1)
    fold = jnp.where((lane_i >> 4) == (lane_j & 7), 1.0, 0.0).astype(F32)
    unfold = jnp.where((lane_i & 7) == (lane_j >> 4), 1.0, 0.0).astype(F32)
    own_lanes = lax.broadcasted_iota(jnp.int32, (8, 128), 0) == (
        lax.broadcasted_iota(jnp.int32, (8, 128), 1) >> 3
    )

    def fold_groups(first, second):
        parts = [v[:, 128 * k : 128 * k + 128] for v in (first, second) for k in range(4)]
        tile = jnp.concatenate(parts, axis=0)
        sums = jnp.dot(tile, fold, precision=lax.Precision.HIGHEST, preferred_element_type=F32)
        return jnp.sum(jnp.where(own_lanes, sums, 0.0), axis=0, keepdims=True)

    def unfold_groups(row):
        tile = jnp.where(own_lanes, jnp.broadcast_to(row, (8, 128)), 0.0)
        return jnp.dot(tile, unfold, precision=lax.Precision.HIGHEST, preferred_element_type=F32)

    loads[2].wait()
    first = jnp.zeros((16, 512), F32)
    second = jnp.zeros((16, 512), F32)
    for f in range(3):
        for r in range(4):
            live = jnp.where((f < fl) & (r < rl), 1.0, 0.0).astype(F32)
            value = y_ref[f, r].astype(F32) * live
            first = first + value
            second = second + value * value
    stats = fold_groups(jnp.sum(first, axis=0, keepdims=True), jnp.sum(second, axis=0, keepdims=True))
    for load in loads[3:]:
        load.wait()

    def table(role):
        t0, taps = TAPS[role]
        half = taps // 2
        t = Table(send0 if role == 0 else send1, recv0 if role == 0 else recv1)

        def piece(column, block, lo=0, n=taps):
            row = pl.multiple_of(block * 32, 32)
            return whole.at[pl.ds(t0 + lo, n), column, pl.ds(row, 32)]

        lane = pl.multiple_of(x * 128, 128)
        src = mine.at[pl.ds(t0, taps), :, pl.ds(lane, 128)]
        place = slots.at[pl.ds(0, taps), h * 2 + c]
        for d in range(1, 4):
            device = at(z_=mod(z + (2 * zl - 1) * d, 8), c_=role)
            t.add(f"a{d}0", src, place, device)
            t.add(f"a{d}1", src, place, device)
        t.add("as", src, place, at(c_=role))
        columns = [x, mod(x - 1, 4), mod(x + 1, 4), mod(x + 2, 4)]
        blocks = [y]
        for s in range(1, 4):
            blocks += [mod(y - s, 8), mod(y + s, 8)]
        blocks.append(mod(y + 4, 8))
        left, right = at(x_=mod(x - 1, 4)), at(x_=mod(x + 1, 4))
        up, down = at(y_=mod(y + 1, 8)), at(y_=mod(y - 1, 8))
        parts = ((0, half), (half, taps - half))
        for k in range(8 if role == 0 else 1):
            for q in (0, 1):
                ref = piece(columns[0], blocks[k], *parts[q])
                t.add(f"xr{k}{q}", ref, ref, right)
                t.add(f"xl{k}{q}", ref, ref, left)
            ref = piece(columns[1], blocks[k], *parts[0])
            t.add(f"or{k}", ref, ref, right)
            ref = piece(columns[2], blocks[k], *parts[1])
            t.add(f"ol{k}", ref, ref, left)
        for j in range(1 if role == 0 else 4):
            for s in range(4):
                for q in (0, 1):
                    if s < 3 or q == 0:
                        ref = piece(columns[j], mod(y - s, 8), *parts[q])
                        t.add(f"yp{j}{s}{q}", ref, ref, up)
                    if s < 3 or q == 1:
                        ref = piece(columns[j], mod(y + s, 8), *parts[q])
                        t.add(f"ym{j}{s}{q}", ref, ref, down)
        for k in range(8):
            for j in range(4):
                ref = piece(columns[j], blocks[k])
                t.add(f"d{k}{j}", ref, ref, at(c_=1 - role))
        return t

    tables = (table(0), table(1))

    def stage_a_send():
        for role in (0, 1):
            @pl.when(c == 0)
            def _():
                for d in range(1, 4):
                    tables[role].start(f"a{d}0")

            @pl.when(c == 1)
            def _():
                for d in range(1, 4):
                    tables[role].start(f"a{d}1")

            @pl.when(c == 1 - role)
            def _():
                tables[role].start("as")

    def stage_a_sent():
        for role in (0, 1):
            @pl.when(c == 0)
            def _():
                for d in range(1, 4):
                    tables[role].sent(f"a{d}0")

            @pl.when(c == 1)
            def _():
                for d in range(1, 4):
                    tables[role].sent(f"a{d}1")

            @pl.when(c == 1 - role)
            def _():
                tables[role].sent("as")

    def stage_a_arrive(role):
        t0, taps = TAPS[role]
        t = tables[role]
        lane = pl.multiple_of(x * 128, 128)
        slots[0:taps, h * 2 + role] = mine[t0 : t0 + taps, :, pl.ds(lane, 128)]
        for d in range(1, 4):
            t.arrive(f"a{d}0", f"a{d}1")
        t.arrive("as")
        row = pl.multiple_of(y * 32, 32)
        for s in range(8):
            rows32[0:taps, 4 * s : 4 * s + 4] = slots[0:taps, s].astype(F32)
        whole[t0 : t0 + taps, x, pl.ds(row, 32)] = rows32[0:taps].astype(BF)

    def begin(role):
        t = tables[role]
        for q in (0, 1):
            both = [f"yp00{q}", f"ym00{q}", f"xr0{q}", f"xl0{q}"]
            t.start(*(both if role == 0 else both[2:] + both[:2]))
        t.start("d00")

    def x_in0(k):
        t = tables[0]
        t.arrive(f"xr{k}0")
        t.start(f"or{k}")
        t.arrive(f"xl{k}1")
        t.start(f"ol{k}")
        t.arrive(f"xr{k}1")
        t.start(f"d{k}1")
        t.arrive(f"xl{k}0")
        t.start(f"d{k}2")

    def o_in0(k):
        t = tables[0]
        t.arrive(f"or{k}", f"ol{k}")
        t.start(f"d{k}3")

    def y_in0(s):
        t = tables[0]
        k = 2 * s - 1
        for q in (0, 1):
            if s < 4 or q == 0:
                t.arrive(f"yp0{s - 1}{q}")
                if s < 3 or (s == 3 and q == 0):
                    t.start(f"yp0{s}{q}")
                t.start(f"xr{k}{q}", f"xl{k}{q}")
            if s < 4 or q == 1:
                t.arrive(f"ym0{s - 1}{q}")
                if s < 3 or (s == 3 and q == 1):
                    t.start(f"ym0{s}{q}")
                m = min(k + 1, 7)
                t.start(f"xr{m}{q}", f"xl{m}{q}")
        t.start(f"d{k}0")
        if s < 4:
            t.start(f"d{k + 1}0")

    def x_in1():
        t = tables[1]
        for q in (0, 1):
            t.arrive(f"xr0{q}")
            t.start(f"yp10{q}", f"ym10{q}")
            if q == 0:
                t.start("or0")
        for q in (1, 0):
            t.arrive(f"xl0{q}")
            if q == 1:
                t.start("ol0")
            t.start(f"yp20{q}", f"ym20{q}")
        t.start("d01", "d02")

    def o_in1():
        t = tables[1]
        t.arrive("or0")
        t.start("yp300", "ym300")
        t.arrive("ol0")
        t.start("yp301", "ym301", "d03")

    def y_in1(s, chains=(0, 1, 2, 3)):
        t = tables[1]
        for j in chains:
            for q in (0, 1):
                if s < 4 or q == 0:
                    t.arrive(f"yp{j}{s - 1}{q}")
                    if s < 3 or (s == 3 and q == 0):
                        t.start(f"yp{j}{s}{q}")
                if s < 4 or q == 1:
                    t.arrive(f"ym{j}{s - 1}{q}")
                    if s < 3 or (s == 3 and q == 1):
                        t.start(f"ym{j}{s}{q}")
            t.start(f"d{2 * s - 1}{j}")
            if s < 4:
                t.start(f"d{2 * s}{j}")

    def small_copy(which):
        before, sibling = (mod(tm - 1, 64), height), at(c_=1 - c)
        if which == 0:
            src, dst, device = g_ref.at[pl.ds(0, 2)], ahead.at[pl.ds(0, 2)], sibling
        elif which == 1:
            src, dst, device = g_ref.at[0], ahead.at[0], before
        elif which == 2:
            src, dst, device = chosen_next, ahead.at[1], before
        elif which == 3:
            src, dst, device = ahead.at[0], ahead.at[2], sibling
        elif which == 4:
            src, dst, device = edge_out.at[1], edge_in.at[0], (tm, mod(height + 1, 8))
        else:
            src, dst, device = edge_out.at[0], edge_in.at[1], (tm, mod(height - 1, 8))
        return pltpu.make_async_remote_copy(
            src_ref=src, dst_ref=dst, send_sem=small_send.at[which], recv_sem=small_recv.at[which],
            device_id=device, device_id_type=pl.DeviceIdType.MESH,
        )

    zero_frame = jnp.zeros((8, 32, 256), BF)
    zero_row = jnp.zeros((32, 256), BF)

    def frames_begin():
        @pl.when(c == 0)
        def _():
            small_copy(1).start()

        @pl.when(c == 1)
        def _():
            small_copy(0).start()

    def frames_choose():
        @pl.when(c == 0)
        def _():
            small_copy(0).wait_recv()
            chosen_next[...] = lax.select(fl >= 2, g_ref[1], ahead[0])
            small_copy(2).start()

    def frames_pass():
        @pl.when(c == 1)
        def _():
            small_copy(1).wait_recv()
            small_copy(3).start()

    def order_frames():
        @pl.when(c == 0)
        def _():
            small_copy(3).wait_recv()

        @pl.when(c == 1)
        def _():
            small_copy(2).wait_recv()

        has_one = tm < 63
        has_two = jnp.logical_and(has_one, jnp.logical_or(fl_next >= 2, tm < 62))
        following = lax.select(has_one, ahead[0], zero_frame)
        after = lax.select(jnp.logical_or(c == 1, fl_next >= 2), ahead[1], ahead[2])
        after = lax.select(has_two, after, zero_frame)
        own = [g_ref[0], g_ref[1], g_ref[2]]
        ordered = [
            own[0],
            lax.select(fl >= 2, own[1], following),
            lax.select(fl >= 3, own[2], lax.select(fl == 2, following, after)),
            lax.select(fl >= 3, following, lax.select(fl == 2, after, zero_frame)),
            lax.select(fl >= 3, after, zero_frame),
        ]
        for p in range(5):
            last = ordered[p][1]
            for r in range(8):
                row = ordered[p][r]
                if r >= 2:
                    row = lax.select(r < 2 * rl, row, zero_row)
                if r >= 3 and r % 2 == 1:
                    last = lax.select(r == 2 * rl - 1, row, last)
                padded[p, r + 1] = row
            edge_out[0, p] = ordered[p][0]
            edge_out[1, p] = last
        small_copy(4).start()
        small_copy(5).start()

    def finish_rows():
        small_copy(4).wait_recv()
        small_copy(5).wait_recv()
        for p in range(5):
            above = lax.select(height > 0, edge_in[0, p], zero_row)
            below = lax.select(height < 7, edge_in[1, p], zero_row)
            padded[p, 0] = above
            for r in (2, 4, 6):
                padded[p, r + 1] = lax.select(r == 2 * rl, below, padded[p, r + 1])
            padded[p, 9] = lax.select(rl == 4, below, zero_row)

    def make_windows():
        out_row = lax.broadcasted_iota(jnp.int32, (64, 320), 0)
        in_row = lax.broadcasted_iota(jnp.int32, (64, 320), 1)
        down_by = (in_row >> 5) - 2 * (out_row >> 4)
        along_by = (in_row & 31) - 2 * (out_row & 15)
        choose = []
        for kh in range(3):
            for kw in range(3):
                dr, dc = down_by - (2 - kh), along_by - (1 - kw)
                hit = ((dr == 0) | (dr == 1)) & ((dc == 0) | (dc == 1))
                choose.append(jnp.where(hit, 1.0, 0.0).astype(F32))
        chosen = jnp.concatenate(choose, axis=0).astype(BF)

        def one(f, carry):
            total = jnp.dot(chosen, padded[f].reshape(320, 256), preferred_element_type=F32)
            top = total.astype(BF)
            rest = (total - top.astype(F32)).astype(BF)
            windows[f, 0] = top.reshape(9, 64, 256)
            windows[f, 1] = rest.reshape(9, 64, 256)
            return carry

        lax.fori_loop(0, 5, one, 0)

    def make_slope(total):
        gs = unfold_groups(total) * (1.0 / COUNT)
        mean, msq = gs[0:4], gs[4:8]
        rstd = lax.rsqrt(msq - mean * mean + EPSILON)
        mean_row, rstd_row = row_of(mean, 0), row_of(rstd, 0)
        gain, bias = gain_ref[...], bias_ref[...]

        def one(i, carry):
            value = (y_ref[i // 4, lax.rem(i, 4)].astype(F32) - mean_row) * rstd_row
            pre = value * gain + bias
            sig = jax.nn.sigmoid(pre)
            hat[i] = value
            slope[i] = sig * (1.0 + pre * (1.0 - sig)) * gain
            return carry

        lax.fori_loop(0, 12, one, 0)
        return rstd_row

    pl.semaphore_wait(barrier, len(partners))
    stage_a_send()
    frames_begin()
    ar_begin(0, 0, stats)
    frames_choose()

    @pl.when(c == 0)
    def _():
        stage_a_arrive(0)
        begin(0)

    @pl.when(c == 1)
    def _():
        stage_a_arrive(1)
        begin(1)

    ar_begin(0, 1, ar_end(0, 0))
    frames_pass()

    @pl.when(c == 0)
    def _():
        y_in0(1)
        x_in0(0)

    @pl.when(c == 1)
    def _():
        x_in1()

    rstd_row = make_slope(ar_end(0, 1))

    @pl.when(c == 0)
    def _():
        y_in0(2)
        x_in0(1)
        o_in0(0)
        x_in0(2)

    @pl.when(c == 1)
    def _():
        y_in1(1, (0,))
        o_in1()
        y_in1(1, (1, 2))

    order_frames()

    @pl.when(c == 0)
    def _():
        y_in0(3)
        o_in0(1)
        x_in0(3)
        o_in0(2)
        x_in0(4)
        y_in0(4)

    @pl.when(c == 1)
    def _():
        y_in1(1, (3,))
        y_in1(2)

    finish_rows()
    make_windows()

    @pl.when(c == 0)
    def _():
        o_in0(3)
        x_in0(5)
        o_in0(4)
        x_in0(6)
        o_in0(5)
        x_in0(7)
        o_in0(6)
        for k in range(8):
            tables[1].arrive(*[f"d{k}{j}" for j in range(4)])

    @pl.when(c == 1)
    def _():
        y_in1(3)
        y_in1(4)

    def kernel_rows(first_tap, n):
        block = whole[pl.ds(first_tap, n)]
        return jnp.concatenate([block[:, k].reshape(n * 256, 128) for k in range(4)], axis=1)

    def taps_of(i, carry):
        kt, kh = i // 3, lax.rem(i, 3)
        lhs = jnp.concatenate(
            [windows[pl.ds(2 - kt, 3), :, kh * 3 + kw].reshape(384, 256) for kw in range(3)], axis=1
        )
        acc[...] += jnp.dot(lhs, kernel_rows(3 * i, 3), preferred_element_type=F32).reshape(3, 2, 64, 512)
        return carry

    skip[...] = jnp.dot(
        windows[0:3, :, 4].reshape(384, 256), kernel_rows(27, 1), preferred_element_type=F32
    ).reshape(3, 2, 64, 512)
    acc[...] = jnp.zeros_like(acc)
    lax.fori_loop(TAPS[1][0] // 3, 9, taps_of, 0)

    @pl.when(c == 0)
    def _():
        o_in0(7)

    @pl.when(c == 1)
    def _():
        for k in range(8):
            tables[0].arrive(*[f"d{k}{j}" for j in range(4)])

    lax.fori_loop(0, TAPS[1][0] // 3, taps_of, 0)

    one_sum = jnp.zeros((16, 512), F32)
    two_sum = jnp.zeros((16, 512), F32)
    for f in range(3):
        for r in range(4):
            here = slice(16 * r, 16 * r + 16)
            live = jnp.where((f < fl) & (r < rl), 1.0, 0.0).astype(F32)
            grad = (acc[f, 0, here] + acc[f, 1, here]) * slope[4 * f + r]
            slope[4 * f + r] = grad
            one_sum = one_sum + grad * live
            two_sum = two_sum + grad * hat[4 * f + r] * live
    sums = fold_groups(jnp.sum(one_sum, axis=0, keepdims=True), jnp.sum(two_sum, axis=0, keepdims=True))
    ar_begin(1, 0, sums)
    ar_begin(1, 1, ar_end(1, 0))
    both = unfold_groups(ar_end(1, 1)) * (1.0 / COUNT)
    b_one, b_two = row_of(both, 0), row_of(both, 4)
    for f in range(3):
        for r in range(4):
            here = slice(16 * r, 16 * r + 16)
            live = jnp.where((f < fl) & (r < rl), 1.0, 0.0).astype(F32)
            value = rstd_row * (slope[4 * f + r] - (b_one + hat[4 * f + r] * b_two))
            out_ref[f, r] = (value + (skip[f, 0, here] + skip[f, 1, here])) * live

    stage_a_sent()
    for role, sent_by in ((0, (1, 2)), (1, (0, 3))):
        @pl.when(c == role)
        def _():
            for which in sent_by:
                small_copy(which).wait_send()
    for which in (4, 5):
        small_copy(which).wait_send()
    for turn in range(2):
        for step in range(2):
            for k in range((31, 15)[step]):
                ar_copy(turn, step, k).wait_send()
    for role in (0, 1):
        @pl.when(c == role)
        def _():
            tables[role].sent(*[n for n in tables[role].entries if n[0] != "a"])


def shards(coarse_input, cotangent, conv_kernel, short_kernel, norm_gain, norm_bias, frame_lengths, row_lengths):
    vmem = pl.BlockSpec(memory_space=pltpu.VMEM)
    anywhere = pl.BlockSpec(memory_space=pl.ANY)
    copies = (7 + 48 + 14 + 32, 7 + 6 + 56 + 32)
    return pl.pallas_call(
        kernel,
        out_shape=jax.ShapeDtypeStruct((3, 4, 16, 512), F32),
        in_specs=[anywhere] * 8,
        out_specs=vmem,
        scratch_shapes=[
            pltpu.SMEM((64,), jnp.int32),
            pltpu.SMEM((8,), jnp.int32),
            pltpu.VMEM((3, 4, 16, 512), BF),
            pltpu.VMEM((3, 8, 32, 256), BF),
            pltpu.VMEM((1, 512), F32),
            pltpu.VMEM((1, 512), F32),
            pltpu.SemaphoreType.DMA((8,)),
            pltpu.VMEM((28, 4, 256, 128), BF),
            pltpu.VMEM((28, 4, 512), BF),
            pltpu.VMEM((18, 8, 4, 128), BF),
            pltpu.VMEM((18, 32, 128), F32),
            pltpu.VMEM((3, 8, 32, 256), BF),
            pltpu.VMEM((8, 32, 256), BF),
            pltpu.VMEM((2, 5, 32, 256), BF),
            pltpu.VMEM((2, 5, 32, 256), BF),
            pltpu.VMEM((5, 10, 32, 256), BF),
            pltpu.VMEM((5, 2, 9, 64, 256), BF),
            pltpu.VMEM((3, 2, 64, 512), F32),
            pltpu.VMEM((3, 2, 64, 512), F32),
            pltpu.VMEM((12, 16, 512), F32),
            pltpu.VMEM((12, 16, 512), F32),
            pltpu.VMEM((2, 32, 1, 128), F32),
            pltpu.VMEM((2, 16, 1, 128), F32),
            pltpu.SemaphoreType.DMA((2, 31)),
            pltpu.SemaphoreType.DMA((2, 31)),
            pltpu.SemaphoreType.DMA((2, 15)),
            pltpu.SemaphoreType.DMA((2, 15)),
            pltpu.SemaphoreType.DMA((6,)),
            pltpu.SemaphoreType.DMA((6,)),
            pltpu.SemaphoreType.DMA((copies[0],)),
            pltpu.SemaphoreType.DMA((copies[0],)),
            pltpu.SemaphoreType.DMA((copies[1],)),
            pltpu.SemaphoreType.DMA((copies[1],)),
        ],
        compiler_params=pltpu.CompilerParams(
            collective_id=0, has_side_effects=True, vmem_limit_bytes=60 * 1024 * 1024
        ),
    )(
        frame_lengths, row_lengths, coarse_input, cotangent,
        conv_kernel.transpose(0, 2, 1), short_kernel.transpose(0, 2, 1),
        norm_gain.reshape(1, 512), norm_bias.reshape(1, 512),
    )


def solution(mesh):
    return jax.shard_map(
        shards,
        mesh=mesh,
        in_specs=(
            P("tm", "height", None, None),
            P("tm", "height", None, None),
            P(None, None, "tm"),
            P(None, None, "tm"),
            P(),
            P(),
            P(),
            P(),
        ),
        out_specs=P("tm", "height", None, None),
        check_vma=False,
    )
```

```python
import functools

import jax
import jax.numpy as jnp
from jax import lax
from jax.experimental import pallas as pl
from jax.experimental.pallas import tpu as pltpu
from jax.sharding import PartitionSpec as P

EPSILON = 1e-06
COUNT = 422144.0
TAPS = ((0, 16), (16, 12))
BF = jnp.bfloat16
F32 = jnp.float32


def mod(value, n):
    return lax.rem(value + n, n)


class Table:
    def __init__(self, send, recv):
        self.send, self.recv, self.entries, self.count = send, recv, {}, 0

    def add(self, name, src, dst, device):
        self.entries[name] = (src, dst, device, self.count)
        self.count += 1

    def get(self, name):
        src, dst, device, at = self.entries[name]
        return pltpu.make_async_remote_copy(
            src_ref=src() if callable(src) else src,
            dst_ref=dst() if callable(dst) else dst,
            send_sem=self.send.at[at],
            recv_sem=self.recv.at[at],
            device_id=device,
            device_id_type=pl.DeviceIdType.MESH,
        )

    def start(self, *names):
        for name in names:
            self.get(name).start()

    def arrive(self, *names):
        for name in names:
            self.get(name).wait_recv()

    def sent(self, *names):
        for name in names:
            self.get(name).wait_send()


def ring_distance(d, n):
    return min(d, n - d)


PLANE = sorted(
    [(dx, dy) for dx in range(4) for dy in range(8) if dx + dy],
    key=lambda d: -(ring_distance(d[0], 4) + ring_distance(d[1], 8)),
)
COLUMN = sorted(
    [(dz, dc) for dz in range(8) for dc in range(2) if dz + dc],
    key=lambda d: -(ring_distance(d[0], 8) + d[1]),
)


def kernel(
    fl_any, rl_any, y_any, g_any, wc_any, ws_any, gain_any, bias_any, out_ref,
    fl_ref, rl_ref, y_ref, g_ref, gain_ref, bias_ref, load_sem,
    whole, mine, slots, rows32, ahead, chosen_next, edge_out, edge_in, padded, chosen, windows,
    acc, skip, hat, slope, plane, column, plane_send, plane_recv, column_send, column_recv,
    small_send, small_recv, send0, recv0, send1, recv1,
):
    tm, height = lax.axis_index("tm"), lax.axis_index("height")
    y, h, c = tm // 8, lax.rem(tm // 2, 4), lax.rem(tm, 2)
    x, zl = height // 2, lax.rem(height, 2)
    z = h * 2 + zl

    def at(y_=y, z_=z, c_=c, x_=x):
        return (y_ * 8 + (z_ // 2) * 2 + c_, x_ * 2 + lax.rem(z_, 2))

    def plane_device(d):
        return at(x_=lax.rem(x + d[0], 4), y_=lax.rem(y + d[1], 8))

    def column_device(d):
        return at(z_=lax.rem(z + d[0], 8), c_=lax.rem(c + d[1], 2))

    partners = [plane_device(d) for d in PLANE] + [column_device(d) for d in COLUMN]
    for d in (1, 2, 62, 63):
        partners.append((lax.rem(tm + d, 64), height))
    for d in (1, 7):
        partners.append((tm, lax.rem(height + d, 8)))
    barrier = pltpu.get_barrier_semaphore()
    for partner in partners:
        pl.semaphore_signal(barrier, inc=1, device_id=partner, device_id_type=pl.DeviceIdType.MESH)
    loads = [
        pltpu.make_async_copy(src, dst, load_sem.at[k])
        for k, (src, dst) in enumerate((
            (wc_any, mine.at[pl.ds(0, 27)]), (ws_any, mine.at[pl.ds(27, 1)]), (g_any, g_ref), (fl_any, fl_ref),
            (rl_any, rl_ref), (y_any, y_ref), (gain_any, gain_ref), (bias_any, bias_ref),
        ))
    ]
    for load in loads:
        load.start()

    def ar_copy(turn, step, k):
        if step == 0:
            place, device = plane.at[turn, x * 8 + y], plane_device(PLANE[k])
            sems = plane_send.at[turn, k], plane_recv.at[turn, k]
        else:
            place, device = column.at[turn, z * 2 + c], column_device(COLUMN[k])
            sems = column_send.at[turn, k], column_recv.at[turn, k]
        return pltpu.make_async_remote_copy(
            src_ref=place, dst_ref=place, send_sem=sems[0], recv_sem=sems[1],
            device_id=device, device_id_type=pl.DeviceIdType.MESH,
        )

    def ar_begin(turn, step, value):
        if step == 0:
            plane[turn, x * 8 + y] = value
        else:
            column[turn, z * 2 + c] = value
        for k in range((31, 15)[step]):
            ar_copy(turn, step, k).start()

    def ar_end(turn, step):
        for k in range((31, 15)[step]):
            ar_copy(turn, step, k).wait_recv()
        return jnp.sum((plane, column)[step][turn], axis=0)

    def row_of(tile, base):
        return jnp.concatenate([tile[base + k : base + k + 1] for k in range(4)], axis=1)

    lane_i = lax.broadcasted_iota(jnp.int32, (128, 128), 0)
    lane_j = lax.broadcasted_iota(jnp.int32, (128, 128), 1)
    fold = jnp.where((lane_i >> 4) == (lane_j & 7), 1.0, 0.0).astype(F32)
    unfold = jnp.where((lane_i & 7) == (lane_j >> 4), 1.0, 0.0).astype(F32)
    own_lanes = lax.broadcasted_iota(jnp.int32, (8, 128), 0) == (
        lax.broadcasted_iota(jnp.int32, (8, 128), 1) >> 3
    )

    def fold_groups(first, second):
        parts = [v[:, 128 * k : 128 * k + 128] for v in (first, second) for k in range(4)]
        tile = jnp.concatenate(parts, axis=0)
        sums = jnp.dot(tile, fold, precision=lax.Precision.HIGHEST, preferred_element_type=F32)
        return jnp.sum(jnp.where(own_lanes, sums, 0.0), axis=0, keepdims=True)

    def unfold_groups(row):
        tile = jnp.where(own_lanes, jnp.broadcast_to(row, (8, 128)), 0.0)
        return jnp.dot(tile, unfold, precision=lax.Precision.HIGHEST, preferred_element_type=F32)

    def table(role):
        t0, taps = TAPS[role]
        half = taps // 2
        t = Table(send0 if role == 0 else send1, recv0 if role == 0 else recv1)

        def piece(column, block, lo=0, n=taps):
            row = pl.multiple_of(block * 32, 32)
            return whole.at[pl.ds(t0 + lo, n), column, pl.ds(row, 32)]

        lane = pl.multiple_of(x * 128, 128)
        src = mine.at[pl.ds(t0, taps), :, pl.ds(lane, 128)]
        place = slots.at[pl.ds(0, taps), h * 2 + c]
        for d in range(1, 4):
            device = at(z_=mod(z + (2 * zl - 1) * d, 8), c_=role)
            t.add(f"a{d}0", src, place, device)
            t.add(f"a{d}1", src, place, device)
        t.add("as", src, place, at(c_=role))
        columns = [x, mod(x - 1, 4), mod(x + 1, 4), mod(x + 2, 4)]
        blocks = [y]
        for s in range(1, 4):
            blocks += [mod(y - s, 8), mod(y + s, 8)]
        blocks.append(mod(y + 4, 8))
        left, right = at(x_=mod(x - 1, 4)), at(x_=mod(x + 1, 4))
        up, down = at(y_=mod(y + 1, 8)), at(y_=mod(y - 1, 8))
        parts = ((0, half), (half, taps - half))
        for k in range(8 if role == 0 else 1):
            for q in (0, 1):
                ref = piece(columns[0], blocks[k], *parts[q])
                t.add(f"xr{k}{q}", ref, ref, right)
                t.add(f"xl{k}{q}", ref, ref, left)
            ref = piece(columns[1], blocks[k], *parts[0])
            t.add(f"or{k}", ref, ref, right)
            ref = piece(columns[2], blocks[k], *parts[1])
            t.add(f"ol{k}", ref, ref, left)
        for j in range(1 if role == 0 else 4):
            for s in range(4):
                for q in (0, 1):
                    if s < 3 or q == 0:
                        ref = piece(columns[j], mod(y - s, 8), *parts[q])
                        t.add(f"yp{j}{s}{q}", ref, ref, up)
                    if s < 3 or q == 1:
                        ref = piece(columns[j], mod(y + s, 8), *parts[q])
                        t.add(f"ym{j}{s}{q}", ref, ref, down)
        for k in range(8):
            for j in range(4):
                ref = piece(columns[j], blocks[k])
                t.add(f"d{k}{j}", ref, ref, at(c_=1 - role))
        return t

    tables = (table(0), table(1))

    def stage_a_send():
        for role in (0, 1):
            @pl.when(c == 0)
            def _():
                for d in range(1, 4):
                    tables[role].start(f"a{d}0")

            @pl.when(c == 1)
            def _():
                for d in range(1, 4):
                    tables[role].start(f"a{d}1")

            @pl.when(c == 1 - role)
            def _():
                tables[role].start("as")

    def stage_a_sent():
        for role in (0, 1):
            @pl.when(c == 0)
            def _():
                for d in range(1, 4):
                    tables[role].sent(f"a{d}0")

            @pl.when(c == 1)
            def _():
                for d in range(1, 4):
                    tables[role].sent(f"a{d}1")

            @pl.when(c == 1 - role)
            def _():
                tables[role].sent("as")

    def stage_a_arrive(role):
        t0, taps = TAPS[role]
        t = tables[role]
        lane = pl.multiple_of(x * 128, 128)
        slots[0:taps, h * 2 + role] = mine[t0 : t0 + taps, :, pl.ds(lane, 128)]
        for d in range(1, 4):
            t.arrive(f"a{d}0", f"a{d}1")
        t.arrive("as")
        row = pl.multiple_of(y * 32, 32)
        for s in range(8):
            rows32[0:taps, 4 * s : 4 * s + 4] = slots[0:taps, s].astype(F32)
        whole[t0 : t0 + taps, x, pl.ds(row, 32)] = rows32[0:taps].astype(BF)

    def begin(role):
        t = tables[role]
        for q in (0, 1):
            both = [f"yp00{q}", f"ym00{q}", f"xr0{q}", f"xl0{q}"]
            t.start(*(both if role == 0 else both[2:] + both[:2]))
        t.start("d00")

    def x_in0(k):
        t = tables[0]
        t.arrive(f"xr{k}0")
        t.start(f"or{k}")
        t.arrive(f"xl{k}1")
        t.start(f"ol{k}")
        t.arrive(f"xr{k}1")
        t.start(f"d{k}1")
        t.arrive(f"xl{k}0")
        t.start(f"d{k}2")

    def o_in0(k):
        t = tables[0]
        t.arrive(f"or{k}", f"ol{k}")
        t.start(f"d{k}3")

    def y_in0(s):
        t = tables[0]
        k = 2 * s - 1
        for q in (0, 1):
            if s < 4 or q == 0:
                t.arrive(f"yp0{s - 1}{q}")
                if s < 3 or (s == 3 and q == 0):
                    t.start(f"yp0{s}{q}")
                t.start(f"xr{k}{q}", f"xl{k}{q}")
            if s < 4 or q == 1:
                t.arrive(f"ym0{s - 1}{q}")
                if s < 3 or (s == 3 and q == 1):
                    t.start(f"ym0{s}{q}")
                m = min(k + 1, 7)
                t.start(f"xr{m}{q}", f"xl{m}{q}")
        t.start(f"d{k}0")
        if s < 4:
            t.start(f"d{k + 1}0")

    def x_in1():
        t = tables[1]
        for q in (0, 1):
            t.arrive(f"xr0{q}")
            t.start(f"yp10{q}", f"ym10{q}")
            if q == 0:
                t.start("or0")
        for q in (1, 0):
            t.arrive(f"xl0{q}")
            if q == 1:
                t.start("ol0")
            t.start(f"yp20{q}", f"ym20{q}")
        t.start("d01", "d02")

    def o_in1():
        t = tables[1]
        t.arrive("or0")
        t.start("yp300", "ym300")
        t.arrive("ol0")
        t.start("yp301", "ym301", "d03")

    def y_in1(s, chains=(0, 1, 2, 3)):
        t = tables[1]
        for j in chains:
            for q in (0, 1):
                if s < 4 or q == 0:
                    t.arrive(f"yp{j}{s - 1}{q}")
                    if s < 3 or (s == 3 and q == 0):
                        t.start(f"yp{j}{s}{q}")
                if s < 4 or q == 1:
                    t.arrive(f"ym{j}{s - 1}{q}")
                    if s < 3 or (s == 3 and q == 1):
                        t.start(f"ym{j}{s}{q}")
            t.start(f"d{2 * s - 1}{j}")
            if s < 4:
                t.start(f"d{2 * s}{j}")

    def small_copy(which):
        before, sibling = (mod(tm - 1, 64), height), at(c_=1 - c)
        if which == 0:
            src, dst, device = g_ref.at[pl.ds(0, 2)], ahead.at[pl.ds(0, 2)], sibling
        elif which == 1:
            src, dst, device = g_ref.at[0], ahead.at[0], before
        elif which == 2:
            src, dst, device = chosen_next, ahead.at[1], before
        elif which == 3:
            src, dst, device = ahead.at[0], ahead.at[2], sibling
        elif which == 4:
            src, dst, device = edge_out.at[1], edge_in.at[0], (tm, mod(height + 1, 8))
        else:
            src, dst, device = edge_out.at[0], edge_in.at[1], (tm, mod(height - 1, 8))
        return pltpu.make_async_remote_copy(
            src_ref=src, dst_ref=dst, send_sem=small_send.at[which], recv_sem=small_recv.at[which],
            device_id=device, device_id_type=pl.DeviceIdType.MESH,
        )

    zero_frame = jnp.zeros((8, 32, 256), BF)
    zero_row = jnp.zeros((32, 256), BF)

    def frames_begin():
        @pl.when(c == 0)
        def _():
            small_copy(1).start()

        @pl.when(c == 1)
        def _():
            small_copy(0).start()

    def frames_choose():
        @pl.when(c == 0)
        def _():
            small_copy(0).wait_recv()
            chosen_next[...] = lax.select(fl >= 2, g_ref[1], ahead[0])
            small_copy(2).start()

    def frames_pass():
        @pl.when(c == 1)
        def _():
            small_copy(1).wait_recv()
            small_copy(3).start()

    def order_frames():
        @pl.when(c == 0)
        def _():
            small_copy(3).wait_recv()

        @pl.when(c == 1)
        def _():
            small_copy(2).wait_recv()

        has_one = tm < 63
        has_two = jnp.logical_and(has_one, jnp.logical_or(fl_next >= 2, tm < 62))
        following = lax.select(has_one, ahead[0], zero_frame)
        after = lax.select(jnp.logical_or(c == 1, fl_next >= 2), ahead[1], ahead[2])
        after = lax.select(has_two, after, zero_frame)
        own = [g_ref[0], g_ref[1], g_ref[2]]
        ordered = [
            own[0],
            lax.select(fl >= 2, own[1], following),
            lax.select(fl >= 3, own[2], lax.select(fl == 2, following, after)),
            lax.select(fl >= 3, following, lax.select(fl == 2, after, zero_frame)),
            lax.select(fl >= 3, after, zero_frame),
        ]
        for p in range(5):
            last = ordered[p][1]
            for r in range(8):
                row = ordered[p][r]
                if r >= 2:
                    row = lax.select(r < 2 * rl, row, zero_row)
                if r >= 3 and r % 2 == 1:
                    last = lax.select(r == 2 * rl - 1, row, last)
                padded[p, r + 1] = row
            edge_out[0, p] = ordered[p][0]
            edge_out[1, p] = last
        small_copy(4).start()
        small_copy(5).start()

    def finish_rows():
        small_copy(4).wait_recv()
        small_copy(5).wait_recv()
        for p in range(5):
            above = lax.select(height > 0, edge_in[0, p], zero_row)
            below = lax.select(height < 7, edge_in[1, p], zero_row)
            padded[p, 0] = above
            for r in (2, 4, 6):
                padded[p, r + 1] = lax.select(r == 2 * rl, below, padded[p, r + 1])
            padded[p, 9] = lax.select(rl == 4, below, zero_row)

    def make_chosen():
        out_row = lax.broadcasted_iota(jnp.int32, (64, 320), 0)
        in_row = lax.broadcasted_iota(jnp.int32, (64, 320), 1)
        down_by = (in_row >> 5) - 2 * (out_row >> 4)
        along_by = (in_row & 31) - 2 * (out_row & 15)
        choose = []
        for kh in range(3):
            for kw in range(3):
                dr, dc = down_by - (2 - kh), along_by - (1 - kw)
                hit = ((dr == 0) | (dr == 1)) & ((dc == 0) | (dc == 1))
                choose.append(jnp.where(hit, 1.0, 0.0).astype(F32))
        chosen[...] = jnp.concatenate(choose, axis=0).astype(BF)

    def make_windows(*frames):
        for f in frames:
            total = jnp.dot(chosen[...], padded[f].reshape(320, 256), preferred_element_type=F32)
            top = total.astype(BF)
            rest = (total - top.astype(F32)).astype(BF)
            windows[f, 0] = top.reshape(9, 64, 256)
            windows[f, 1] = rest.reshape(9, 64, 256)

    def make_slope(total):
        gs = unfold_groups(total) * (1.0 / COUNT)
        mean, msq = gs[0:4], gs[4:8]
        rstd = lax.rsqrt(msq - mean * mean + EPSILON)
        mean_row, rstd_row = row_of(mean, 0), row_of(rstd, 0)
        gain, bias = gain_ref[...], bias_ref[...]

        def one(i, carry):
            value = (y_ref[i // 4, lax.rem(i, 4)].astype(F32) - mean_row) * rstd_row
            pre = value * gain + bias
            sig = jax.nn.sigmoid(pre)
            hat[i] = value
            slope[i] = sig * (1.0 + pre * (1.0 - sig)) * gain
            return carry

        lax.fori_loop(0, 12, one, 0)
        return rstd_row

    loads[0].wait()
    loads[1].wait()
    pl.semaphore_wait(barrier, len(partners))
    stage_a_send()
    for load in loads[2:]:
        load.wait()
    fl, rl = fl_ref[tm], rl_ref[height]
    fl_next = fl_ref[mod(tm + 1, 64)]

    first = jnp.zeros((16, 512), F32)
    second = jnp.zeros((16, 512), F32)
    for f in range(3):
        for r in range(4):
            live = jnp.where((f < fl) & (r < rl), 1.0, 0.0).astype(F32)
            value = y_ref[f, r].astype(F32) * live
            first = first + value
            second = second + value * value
    stats = fold_groups(jnp.sum(first, axis=0, keepdims=True), jnp.sum(second, axis=0, keepdims=True))
    ar_begin(0, 0, stats)
    make_chosen()

    @pl.when(c == 0)
    def _():
        stage_a_arrive(0)
        begin(0)

    @pl.when(c == 1)
    def _():
        stage_a_arrive(1)
        begin(1)

    frames_begin()
    ar_begin(0, 1, ar_end(0, 0))
    frames_choose()

    @pl.when(c == 0)
    def _():
        y_in0(1)
        x_in0(0)

    @pl.when(c == 1)
    def _():
        x_in1()

    frames_pass()
    rstd_row = make_slope(ar_end(0, 1))

    @pl.when(c == 0)
    def _():
        y_in0(2)
        x_in0(1)
        o_in0(0)
        x_in0(2)

    @pl.when(c == 1)
    def _():
        y_in1(1, (0,))
        o_in1()
        y_in1(1, (1, 2))

    @pl.when(c == 0)
    def _():
        y_in0(3)
        o_in0(1)
        x_in0(3)

    @pl.when(c == 1)
    def _():
        y_in1(1, (3,))
        y_in1(2, (0, 1))

    order_frames()

    @pl.when(c == 0)
    def _():
        o_in0(2)
        x_in0(4)
        y_in0(4)

    @pl.when(c == 1)
    def _():
        y_in1(2, (2, 3))

    finish_rows()

    @pl.when(c == 0)
    def _():
        o_in0(3)
        x_in0(5)

    @pl.when(c == 1)
    def _():
        y_in1(3, (0, 1))

    make_windows(0, 1)

    @pl.when(c == 0)
    def _():
        o_in0(4)
        x_in0(6)

    @pl.when(c == 1)
    def _():
        y_in1(3, (2, 3))

    make_windows(2, 3)

    @pl.when(c == 0)
    def _():
        o_in0(5)
        x_in0(7)

    @pl.when(c == 1)
    def _():
        y_in1(4, (0, 1))

    make_windows(4)

    @pl.when(c == 0)
    def _():
        o_in0(6)
        for k in range(8):
            tables[1].arrive(*[f"d{k}{j}" for j in range(4)])

    @pl.when(c == 1)
    def _():
        y_in1(4, (2, 3))

    def kernel_rows(first_tap, n):
        block = whole[pl.ds(first_tap, n)]
        return jnp.concatenate([block[:, k].reshape(n * 256, 128) for k in range(4)], axis=1)

    def taps_of(i, carry):
        kt, kh = i // 3, lax.rem(i, 3)
        lhs = jnp.concatenate(
            [windows[pl.ds(2 - kt, 3), :, kh * 3 + kw].reshape(384, 256) for kw in range(3)], axis=1
        )
        acc[...] += jnp.dot(lhs, kernel_rows(3 * i, 3), preferred_element_type=F32).reshape(3, 2, 64, 512)
        return carry

    skip[...] = jnp.dot(
        windows[0:3, :, 4].reshape(384, 256), kernel_rows(27, 1), preferred_element_type=F32
    ).reshape(3, 2, 64, 512)
    acc[...] = jnp.zeros_like(acc)
    lax.fori_loop(6, 9, taps_of, 0)

    @pl.when(c == 0)
    def _():
        o_in0(7)

    @pl.when(c == 1)
    def _():
        for k in range(8):
            tables[0].arrive(*[f"d{k}{j}" for j in range(4)])

    lax.fori_loop(0, 6, taps_of, 0)

    one_sum = jnp.zeros((16, 512), F32)
    two_sum = jnp.zeros((16, 512), F32)
    for f in range(3):
        for r in range(4):
            here = slice(16 * r, 16 * r + 16)
            live = jnp.where((f < fl) & (r < rl), 1.0, 0.0).astype(F32)
            grad = (acc[f, 0, here] + acc[f, 1, here]) * slope[4 * f + r]
            slope[4 * f + r] = grad
            one_sum = one_sum + grad * live
            two_sum = two_sum + grad * hat[4 * f + r] * live
    sums = fold_groups(jnp.sum(one_sum, axis=0, keepdims=True), jnp.sum(two_sum, axis=0, keepdims=True))
    ar_begin(1, 0, sums)
    stage_a_sent()
    for role, sent_by in ((0, (1, 2)), (1, (0, 3))):
        @pl.when(c == role)
        def _():
            for which in sent_by:
                small_copy(which).wait_send()
            tables[role].sent(*[n for n in tables[role].entries if n[0] != "a"])
    for which in (4, 5):
        small_copy(which).wait_send()
    for step in range(2):
        for k in range((31, 15)[step]):
            ar_copy(0, step, k).wait_send()
    ar_begin(1, 1, ar_end(1, 0))
    for k in range(31):
        ar_copy(1, 0, k).wait_send()
    both = unfold_groups(ar_end(1, 1)) * (1.0 / COUNT)
    b_one, b_two = row_of(both, 0), row_of(both, 4)
    for f in range(3):
        for r in range(4):
            here = slice(16 * r, 16 * r + 16)
            live = jnp.where((f < fl) & (r < rl), 1.0, 0.0).astype(F32)
            value = rstd_row * (slope[4 * f + r] - (b_one + hat[4 * f + r] * b_two))
            out_ref[f, r] = (value + (skip[f, 0, here] + skip[f, 1, here])) * live
    for k in range(15):
        ar_copy(1, 1, k).wait_send()


def shards(coarse_input, cotangent, conv_kernel, short_kernel, norm_gain, norm_bias, frame_lengths, row_lengths):
    vmem = pl.BlockSpec(memory_space=pltpu.VMEM)
    anywhere = pl.BlockSpec(memory_space=pl.ANY)
    copies = (7 + 48 + 14 + 32, 7 + 6 + 56 + 32)
    return pl.pallas_call(
        kernel,
        out_shape=jax.ShapeDtypeStruct((3, 4, 16, 512), F32),
        in_specs=[anywhere] * 8,
        out_specs=vmem,
        scratch_shapes=[
            pltpu.SMEM((64,), jnp.int32),
            pltpu.SMEM((8,), jnp.int32),
            pltpu.VMEM((3, 4, 16, 512), BF),
            pltpu.VMEM((3, 8, 32, 256), BF),
            pltpu.VMEM((1, 512), F32),
            pltpu.VMEM((1, 512), F32),
            pltpu.SemaphoreType.DMA((8,)),
            pltpu.VMEM((28, 4, 256, 128), BF),
            pltpu.VMEM((28, 4, 512), BF),
            pltpu.VMEM((17, 8, 4, 128), BF),
            pltpu.VMEM((17, 32, 128), F32),
            pltpu.VMEM((3, 8, 32, 256), BF),
            pltpu.VMEM((8, 32, 256), BF),
            pltpu.VMEM((2, 5, 32, 256), BF),
            pltpu.VMEM((2, 5, 32, 256), BF),
            pltpu.VMEM((5, 10, 32, 256), BF),
            pltpu.VMEM((576, 320), BF),
            pltpu.VMEM((5, 2, 9, 64, 256), BF),
            pltpu.VMEM((3, 2, 64, 512), F32),
            pltpu.VMEM((3, 2, 64, 512), F32),
            pltpu.VMEM((12, 16, 512), F32),
            pltpu.VMEM((12, 16, 512), F32),
            pltpu.VMEM((2, 32, 1, 128), F32),
            pltpu.VMEM((2, 16, 1, 128), F32),
            pltpu.SemaphoreType.DMA((2, 31)),
            pltpu.SemaphoreType.DMA((2, 31)),
            pltpu.SemaphoreType.DMA((2, 15)),
            pltpu.SemaphoreType.DMA((2, 15)),
            pltpu.SemaphoreType.DMA((6,)),
            pltpu.SemaphoreType.DMA((6,)),
            pltpu.SemaphoreType.DMA((copies[0],)),
            pltpu.SemaphoreType.DMA((copies[0],)),
            pltpu.SemaphoreType.DMA((copies[1],)),
            pltpu.SemaphoreType.DMA((copies[1],)),
        ],
        compiler_params=pltpu.CompilerParams(
            collective_id=0, has_side_effects=True, vmem_limit_bytes=60 * 1024 * 1024
        ),
    )(
        frame_lengths, row_lengths, coarse_input, cotangent,
        conv_kernel.transpose(0, 2, 1), short_kernel.transpose(0, 2, 1),
        norm_gain.reshape(1, 512), norm_bias.reshape(1, 512),
    )


def solution(mesh):
    return jax.shard_map(
        shards,
        mesh=mesh,
        in_specs=(
            P("tm", "height", None, None),
            P("tm", "height", None, None),
            P(None, None, "tm"),
            P(None, None, "tm"),
            P(),
            P(),
            P(),
            P(),
        ),
        out_specs=P("tm", "height", None, None),
        check_vma=False,
    )
```

```python
import functools

import jax
import jax.numpy as jnp
from jax import lax
from jax.experimental import pallas as pl
from jax.experimental.pallas import tpu as pltpu
from jax.sharding import PartitionSpec as P

EPSILON = 1e-06
COUNT = 422144.0
TAPS = ((0, 16), (16, 12))
SHARED = 6
BF = jnp.bfloat16
F32 = jnp.float32


def mod(value, n):
    return lax.rem(value + n, n)


class Table:
    def __init__(self, send, recv):
        self.send, self.recv, self.entries, self.count = send, recv, {}, 0

    def add(self, name, src, dst, device):
        self.entries[name] = (src, dst, device, self.count)
        self.count += 1

    def get(self, name):
        src, dst, device, at = self.entries[name]
        return pltpu.make_async_remote_copy(
            src_ref=src() if callable(src) else src,
            dst_ref=dst() if callable(dst) else dst,
            send_sem=self.send.at[at],
            recv_sem=self.recv.at[at],
            device_id=device,
            device_id_type=pl.DeviceIdType.MESH,
        )

    def start(self, *names):
        for name in names:
            self.get(name).start()

    def arrive(self, *names):
        for name in names:
            self.get(name).wait_recv()

    def sent(self, *names):
        for name in names:
            self.get(name).wait_send()


def ring_distance(d, n):
    return min(d, n - d)


PLANE = sorted(
    [(dx, dy) for dx in range(4) for dy in range(8) if dx + dy],
    key=lambda d: -(ring_distance(d[0], 4) + ring_distance(d[1], 8)),
)
COLUMN = sorted(
    [(dz, dc) for dz in range(8) for dc in range(2) if dz + dc],
    key=lambda d: -(ring_distance(d[0], 8) + d[1]),
)


def kernel(
    fl_any, rl_any, y_any, g_any, wc_any, ws_any, gain_any, bias_any, out_ref,
    fl_ref, rl_ref, y_ref, g_ref, gain_ref, bias_ref, load_sem,
    whole, mine, slots, rows32, ahead, chosen_next, edge_out, edge_in, padded, chosen, windows,
    acc, skip, hat, slope, plane, column, plane_send, plane_recv, column_send, column_recv,
    small_send, small_recv, send0, recv0, send1, recv1,
):
    tm, height = lax.axis_index("tm"), lax.axis_index("height")
    y, h, c = tm // 8, lax.rem(tm // 2, 4), lax.rem(tm, 2)
    x, zl = height // 2, lax.rem(height, 2)
    z = h * 2 + zl

    def at(y_=y, z_=z, c_=c, x_=x):
        return (y_ * 8 + (z_ // 2) * 2 + c_, x_ * 2 + lax.rem(z_, 2))

    def plane_device(d):
        return at(x_=lax.rem(x + d[0], 4), y_=lax.rem(y + d[1], 8))

    def column_device(d):
        return at(z_=lax.rem(z + d[0], 8), c_=lax.rem(c + d[1], 2))

    partners = [plane_device(d) for d in PLANE] + [column_device(d) for d in COLUMN]
    for d in (1, 2, 62, 63):
        partners.append((lax.rem(tm + d, 64), height))
    for d in (1, 7):
        partners.append((tm, lax.rem(height + d, 8)))
    barrier = pltpu.get_barrier_semaphore()
    for partner in partners:
        pl.semaphore_signal(barrier, inc=1, device_id=partner, device_id_type=pl.DeviceIdType.MESH)
    lanes = pl.ds(pl.multiple_of(x * 128, 128), 128)
    loads = [
        pltpu.make_async_copy(src, dst, load_sem.at[k])
        for k, (src, dst) in enumerate((
            (wc_any.at[:, :, lanes], mine.at[pl.ds(0, 27)]), (ws_any.at[:, :, lanes], mine.at[pl.ds(27, 1)]),
            (g_any, g_ref), (fl_any, fl_ref),
            (rl_any, rl_ref), (y_any, y_ref), (gain_any, gain_ref), (bias_any, bias_ref),
        ))
    ]
    for load in loads:
        load.start()

    def ar_copy(turn, step, k):
        if step == 0:
            place, device = plane.at[turn, x * 8 + y], plane_device(PLANE[k])
            sems = plane_send.at[turn, k], plane_recv.at[turn, k]
        else:
            place, device = column.at[turn, z * 2 + c], column_device(COLUMN[k])
            sems = column_send.at[turn, k], column_recv.at[turn, k]
        return pltpu.make_async_remote_copy(
            src_ref=place, dst_ref=place, send_sem=sems[0], recv_sem=sems[1],
            device_id=device, device_id_type=pl.DeviceIdType.MESH,
        )

    def ar_begin(turn, step, value):
        if step == 0:
            plane[turn, x * 8 + y] = value
        else:
            column[turn, z * 2 + c] = value
        for k in range((31, 15)[step]):
            ar_copy(turn, step, k).start()

    def ar_end(turn, step):
        for k in range((31, 15)[step]):
            ar_copy(turn, step, k).wait_recv()
        return jnp.sum((plane, column)[step][turn], axis=0)

    def row_of(tile, base):
        return jnp.concatenate([tile[base + k : base + k + 1] for k in range(4)], axis=1)

    lane_i = lax.broadcasted_iota(jnp.int32, (128, 128), 0)
    lane_j = lax.broadcasted_iota(jnp.int32, (128, 128), 1)
    fold = jnp.where((lane_i >> 4) == (lane_j & 7), 1.0, 0.0).astype(F32)
    unfold = jnp.where((lane_i & 7) == (lane_j >> 4), 1.0, 0.0).astype(F32)
    own_lanes = lax.broadcasted_iota(jnp.int32, (8, 128), 0) == (
        lax.broadcasted_iota(jnp.int32, (8, 128), 1) >> 3
    )

    def fold_groups(first, second):
        parts = [v[:, 128 * k : 128 * k + 128] for v in (first, second) for k in range(4)]
        tile = jnp.concatenate(parts, axis=0)
        sums = jnp.dot(tile, fold, precision=lax.Precision.HIGHEST, preferred_element_type=F32)
        return jnp.sum(jnp.where(own_lanes, sums, 0.0), axis=0, keepdims=True)

    def unfold_groups(row):
        tile = jnp.where(own_lanes, jnp.broadcast_to(row, (8, 128)), 0.0)
        return jnp.dot(tile, unfold, precision=lax.Precision.HIGHEST, preferred_element_type=F32)

    def table(role):
        t0, taps = TAPS[role]
        half = taps // 2
        t = Table(send0 if role == 0 else send1, recv0 if role == 0 else recv1)

        def piece(column, block, lo=0, n=taps):
            row = pl.multiple_of(block * 32, 32)
            return whole.at[pl.ds(t0 + lo, n), column, pl.ds(row, 32)]

        src = mine.at[pl.ds(t0, taps)]
        place = slots.at[h * 2 + c, pl.ds(0, taps)]
        for d in range(1, 4):
            device = at(z_=mod(z + (2 * zl - 1) * d, 8), c_=role)
            t.add(f"a{d}0", src, place, device)
            t.add(f"a{d}1", src, place, device)
        t.add("as", src, place, at(c_=role))
        columns = [x, mod(x - 1, 4), mod(x + 1, 4), mod(x + 2, 4)]
        blocks = [y]
        for s in range(1, 4):
            blocks += [mod(y - s, 8), mod(y + s, 8)]
        blocks.append(mod(y + 4, 8))
        left, right = at(x_=mod(x - 1, 4)), at(x_=mod(x + 1, 4))
        up, down = at(y_=mod(y + 1, 8)), at(y_=mod(y - 1, 8))
        parts = ((0, half), (half, taps - half))
        for k in range(8 if role == 0 else 1):
            for q in (0, 1):
                ref = piece(columns[0], blocks[k], *parts[q])
                t.add(f"xr{k}{q}", ref, ref, right)
                t.add(f"xl{k}{q}", ref, ref, left)
            ref = piece(columns[1], blocks[k], *parts[0])
            t.add(f"or{k}", ref, ref, right)
            ref = piece(columns[2], blocks[k], *parts[1])
            t.add(f"ol{k}", ref, ref, left)
            if role == 0 and k < SHARED:
                ref = piece(columns[3], blocks[k])
                t.add(f"zo{k}", ref, ref, at(z_=z + 1 - 2 * zl))
        for j in range(1 if role == 0 else 4):
            for s in range(4):
                for q in (0, 1):
                    if s < 3 or q == 0:
                        ref = piece(columns[j], mod(y - s, 8), *parts[q])
                        t.add(f"yp{j}{s}{q}", ref, ref, up)
                    if s < 3 or q == 1:
                        ref = piece(columns[j], mod(y + s, 8), *parts[q])
                        t.add(f"ym{j}{s}{q}", ref, ref, down)
        for k in range(8):
            for j in range(4):
                ref = piece(columns[j], blocks[k])
                t.add(f"d{k}{j}", ref, ref, at(c_=1 - role))
        return t

    tables = (table(0), table(1))

    def stage_a_send():
        for role in (0, 1):
            @pl.when(c == 0)
            def _():
                for d in range(1, 4):
                    tables[role].start(f"a{d}0")

            @pl.when(c == 1)
            def _():
                for d in range(1, 4):
                    tables[role].start(f"a{d}1")

            @pl.when(c == 1 - role)
            def _():
                tables[role].start("as")

    def stage_a_sent():
        for role in (0, 1):
            @pl.when(c == 0)
            def _():
                for d in range(1, 4):
                    tables[role].sent(f"a{d}0")

            @pl.when(c == 1)
            def _():
                for d in range(1, 4):
                    tables[role].sent(f"a{d}1")

            @pl.when(c == 1 - role)
            def _():
                tables[role].sent("as")

    def stage_a_arrive(role):
        t0, taps = TAPS[role]
        t = tables[role]
        slots[h * 2 + role, 0:taps] = mine[t0 : t0 + taps]
        for d in range(1, 4):
            t.arrive(f"a{d}0", f"a{d}1")
        t.arrive("as")
        row = pl.multiple_of(y * 32, 32)
        for s in range(8):
            rows32[0:taps, 4 * s : 4 * s + 4] = slots[s, 0:taps].astype(F32)
        whole[t0 : t0 + taps, x, pl.ds(row, 32)] = rows32[0:taps].astype(BF)

    def begin(role):
        t = tables[role]
        for q in (0, 1):
            both = [f"yp00{q}", f"ym00{q}", f"xr0{q}", f"xl0{q}"]
            t.start(*(both if role == 0 else both[2:] + both[:2]))
        t.start("d00")

    def mine_to_fetch(k, act, otherwise=None):
        if k >= SHARED:
            act()
            return
        pl.when(zl == k % 2)(act)
        if otherwise is not None:
            pl.when(zl != k % 2)(otherwise)

    def x_in0(k):
        t = tables[0]
        t.arrive(f"xr{k}0")
        mine_to_fetch(k, lambda: t.start(f"or{k}"))
        t.arrive(f"xl{k}1")
        mine_to_fetch(k, lambda: t.start(f"ol{k}"))
        t.arrive(f"xr{k}1")
        t.start(f"d{k}1")
        t.arrive(f"xl{k}0")
        t.start(f"d{k}2")

    def o_in0(k):
        t = tables[0]

        def fetched():
            t.arrive(f"or{k}", f"ol{k}")
            if k < SHARED:
                t.start(f"zo{k}")
            t.start(f"d{k}3")

        def given():
            t.arrive(f"zo{k - 2}")
            t.start(f"d{k - 2}3")

        mine_to_fetch(k, fetched)
        if 0 <= k - 2 < SHARED:
            pl.when(zl != k % 2)(given)

    def y_in0(s):
        t = tables[0]
        k = 2 * s - 1
        for q in (0, 1):
            if s < 4 or q == 0:
                t.arrive(f"yp0{s - 1}{q}")
                if s < 3 or (s == 3 and q == 0):
                    t.start(f"yp0{s}{q}")
                t.start(f"xr{k}{q}", f"xl{k}{q}")
            if s < 4 or q == 1:
                t.arrive(f"ym0{s - 1}{q}")
                if s < 3 or (s == 3 and q == 1):
                    t.start(f"ym0{s}{q}")
                m = min(k + 1, 7)
                t.start(f"xr{m}{q}", f"xl{m}{q}")
        t.start(f"d{k}0")
        if s < 4:
            t.start(f"d{k + 1}0")

    def x_in1():
        t = tables[1]
        for q in (0, 1):
            t.arrive(f"xr0{q}")
            t.start(f"yp10{q}", f"ym10{q}")
            if q == 0:
                t.start("or0")
        for q in (1, 0):
            t.arrive(f"xl0{q}")
            if q == 1:
                t.start("ol0")
            t.start(f"yp20{q}", f"ym20{q}")
        t.start("d01", "d02")

    def o_in1():
        t = tables[1]
        t.arrive("or0")
        t.start("yp300", "ym300")
        t.arrive("ol0")
        t.start("yp301", "ym301", "d03")

    def y_in1(s, chains=(0, 1, 2, 3)):
        t = tables[1]
        for j in chains:
            for q in (0, 1):
                if s < 4 or q == 0:
                    t.arrive(f"yp{j}{s - 1}{q}")
                    if s < 3 or (s == 3 and q == 0):
                        t.start(f"yp{j}{s}{q}")
                if s < 4 or q == 1:
                    t.arrive(f"ym{j}{s - 1}{q}")
                    if s < 3 or (s == 3 and q == 1):
                        t.start(f"ym{j}{s}{q}")
            t.start(f"d{2 * s - 1}{j}")
            if s < 4:
                t.start(f"d{2 * s}{j}")

    def small_copy(which):
        before, sibling = (mod(tm - 1, 64), height), at(c_=1 - c)
        if which == 0:
            src, dst, device = g_ref.at[pl.ds(0, 2)], ahead.at[pl.ds(0, 2)], sibling
        elif which == 1:
            src, dst, device = g_ref.at[0], ahead.at[0], before
        elif which == 2:
            src, dst, device = chosen_next, ahead.at[1], before
        elif which == 3:
            src, dst, device = ahead.at[0], ahead.at[2], sibling
        elif which == 4:
            src, dst, device = edge_out.at[1], edge_in.at[0], (tm, mod(height + 1, 8))
        else:
            src, dst, device = edge_out.at[0], edge_in.at[1], (tm, mod(height - 1, 8))
        return pltpu.make_async_remote_copy(
            src_ref=src, dst_ref=dst, send_sem=small_send.at[which], recv_sem=small_recv.at[which],
            device_id=device, device_id_type=pl.DeviceIdType.MESH,
        )

    zero_frame = jnp.zeros((8, 32, 256), BF)
    zero_row = jnp.zeros((32, 256), BF)

    def frames_begin():
        @pl.when(c == 0)
        def _():
            small_copy(1).start()

        @pl.when(c == 1)
        def _():
            small_copy(0).start()

    def frames_choose():
        @pl.when(c == 0)
        def _():
            small_copy(0).wait_recv()
            chosen_next[...] = lax.select(fl >= 2, g_ref[1], ahead[0])
            small_copy(2).start()

    def frames_pass():
        @pl.when(c == 1)
        def _():
            small_copy(1).wait_recv()
            small_copy(3).start()

    def order_frames():
        @pl.when(c == 0)
        def _():
            small_copy(3).wait_recv()

        @pl.when(c == 1)
        def _():
            small_copy(2).wait_recv()

        has_one = tm < 63
        has_two = jnp.logical_and(has_one, jnp.logical_or(fl_next >= 2, tm < 62))
        following = lax.select(has_one, ahead[0], zero_frame)
        after = lax.select(jnp.logical_or(c == 1, fl_next >= 2), ahead[1], ahead[2])
        after = lax.select(has_two, after, zero_frame)
        own = [g_ref[0], g_ref[1], g_ref[2]]
        ordered = [
            own[0],
            lax.select(fl >= 2, own[1], following),
            lax.select(fl >= 3, own[2], lax.select(fl == 2, following, after)),
            lax.select(fl >= 3, following, lax.select(fl == 2, after, zero_frame)),
            lax.select(fl >= 3, after, zero_frame),
        ]
        for p in range(5):
            last = ordered[p][1]
            for r in range(8):
                row = ordered[p][r]
                if r >= 2:
                    row = lax.select(r < 2 * rl, row, zero_row)
                if r >= 3 and r % 2 == 1:
                    last = lax.select(r == 2 * rl - 1, row, last)
                padded[p, r + 1] = row
            edge_out[0, p] = ordered[p][0]
            edge_out[1, p] = last
        small_copy(4).start()
        small_copy(5).start()

    def finish_rows():
        small_copy(4).wait_recv()
        small_copy(5).wait_recv()
        for p in range(5):
            above = lax.select(height > 0, edge_in[0, p], zero_row)
            below = lax.select(height < 7, edge_in[1, p], zero_row)
            padded[p, 0] = above
            for r in (2, 4, 6):
                padded[p, r + 1] = lax.select(r == 2 * rl, below, padded[p, r + 1])
            padded[p, 9] = lax.select(rl == 4, below, zero_row)

    def make_chosen():
        out_row = lax.broadcasted_iota(jnp.int32, (64, 320), 0)
        in_row = lax.broadcasted_iota(jnp.int32, (64, 320), 1)
        down_by = (in_row >> 5) - 2 * (out_row >> 4)
        along_by = (in_row & 31) - 2 * (out_row & 15)
        choose = []
        for kh in range(3):
            for kw in range(3):
                dr, dc = down_by - (2 - kh), along_by - (1 - kw)
                hit = ((dr == 0) | (dr == 1)) & ((dc == 0) | (dc == 1))
                choose.append(jnp.where(hit, 1.0, 0.0).astype(F32))
        chosen[...] = jnp.concatenate(choose, axis=0).astype(BF)

    def make_windows(*frames):
        for f in frames:
            total = jnp.dot(chosen[...], padded[f].reshape(320, 256), preferred_element_type=F32)
            top = total.astype(BF)
            rest = (total - top.astype(F32)).astype(BF)
            windows[f, 0] = top.reshape(9, 64, 256)
            windows[f, 1] = rest.reshape(9, 64, 256)

    def statistics(total):
        gs = unfold_groups(total) * (1.0 / COUNT)
        mean, msq = gs[0:4], gs[4:8]
        rstd = lax.rsqrt(msq - mean * mean + EPSILON)
        mean_row, rstd_row = row_of(mean, 0), row_of(rstd, 0)
        return mean_row, rstd_row

    def make_slope(low, high, mean_row, rstd_row):
        gain, bias = gain_ref[...], bias_ref[...]

        def one(i, carry):
            value = (y_ref[i // 4, lax.rem(i, 4)].astype(F32) - mean_row) * rstd_row
            pre = value * gain + bias
            sig = jax.nn.sigmoid(pre)
            hat[i] = value
            slope[i] = sig * (1.0 + pre * (1.0 - sig)) * gain
            return carry

        lax.fori_loop(low, high, one, 0)

    loads[0].wait()
    loads[1].wait()
    pl.semaphore_wait(barrier, len(partners))
    stage_a_send()
    for load in loads[2:]:
        load.wait()
    fl, rl = fl_ref[tm], rl_ref[height]
    fl_next = fl_ref[mod(tm + 1, 64)]

    first = jnp.zeros((16, 512), F32)
    second = jnp.zeros((16, 512), F32)
    for f in range(3):
        for r in range(4):
            live = jnp.where((f < fl) & (r < rl), 1.0, 0.0).astype(F32)
            value = y_ref[f, r].astype(F32) * live
            first = first + value
            second = second + value * value
    stats = fold_groups(jnp.sum(first, axis=0, keepdims=True), jnp.sum(second, axis=0, keepdims=True))
    ar_begin(0, 0, stats)
    make_chosen()

    @pl.when(c == 0)
    def _():
        stage_a_arrive(0)
        begin(0)

    @pl.when(c == 1)
    def _():
        stage_a_arrive(1)
        begin(1)

    frames_begin()
    ar_begin(0, 1, ar_end(0, 0))
    frames_choose()

    @pl.when(c == 0)
    def _():
        y_in0(1)
        x_in0(0)

    @pl.when(c == 1)
    def _():
        x_in1()
        y_in1(1, (0,))
        o_in1()

    frames_pass()

    @pl.when(c == 0)
    def _():
        y_in0(2)
        x_in0(1)
        o_in0(0)
        x_in0(2)

    @pl.when(c == 1)
    def _():
        y_in1(1, (1, 2, 3))

    @pl.when(c == 0)
    def _():
        y_in0(3)
        o_in0(1)
        x_in0(3)

    @pl.when(c == 1)
    def _():
        y_in1(2, (0, 1))

    order_frames()

    @pl.when(c == 0)
    def _():
        o_in0(2)
        x_in0(4)
        y_in0(4)

    @pl.when(c == 1)
    def _():
        y_in1(2, (2, 3))

    mean_row, rstd_row = statistics(ar_end(0, 1))
    make_slope(0, 6, mean_row, rstd_row)

    @pl.when(c == 0)
    def _():
        o_in0(3)
        x_in0(5)

    @pl.when(c == 1)
    def _():
        y_in1(3, (0, 1))

    finish_rows()
    make_windows(0, 1)

    @pl.when(c == 0)
    def _():
        o_in0(4)
        x_in0(6)

    @pl.when(c == 1)
    def _():
        y_in1(3, (2, 3))

    make_windows(2, 3)

    @pl.when(c == 0)
    def _():
        o_in0(5)
        x_in0(7)

    @pl.when(c == 1)
    def _():
        y_in1(4, (0, 1))

    make_windows(4)
    make_slope(6, 12, mean_row, rstd_row)

    @pl.when(c == 0)
    def _():
        o_in0(6)
        for k in range(8):
            tables[1].arrive(*[f"d{k}{j}" for j in range(4)])

    @pl.when(c == 1)
    def _():
        y_in1(4, (2, 3))

    def kernel_rows(first_tap, n):
        block = whole[pl.ds(first_tap, n)]
        return jnp.concatenate([block[:, k].reshape(n * 256, 128) for k in range(4)], axis=1)

    def taps_of(i, carry):
        kt, kh = i // 3, lax.rem(i, 3)
        lhs = jnp.concatenate(
            [windows[pl.ds(2 - kt, 3), :, kh * 3 + kw].reshape(384, 256) for kw in range(3)], axis=1
        )
        acc[...] += jnp.dot(lhs, kernel_rows(3 * i, 3), preferred_element_type=F32).reshape(3, 2, 64, 512)
        return carry

    skip[...] = jnp.dot(
        windows[0:3, :, 4].reshape(384, 256), kernel_rows(27, 1), preferred_element_type=F32
    ).reshape(3, 2, 64, 512)
    acc[...] = jnp.zeros_like(acc)
    lax.fori_loop(6, 9, taps_of, 0)

    @pl.when(c == 0)
    def _():
        o_in0(7)

    @pl.when(c == 1)
    def _():
        for k in range(8):
            tables[0].arrive(*[f"d{k}{j}" for j in range(4)])

    lax.fori_loop(0, 6, taps_of, 0)

    one_sum = jnp.zeros((16, 512), F32)
    two_sum = jnp.zeros((16, 512), F32)
    for f in range(3):
        for r in range(4):
            here = slice(16 * r, 16 * r + 16)
            live = jnp.where((f < fl) & (r < rl), 1.0, 0.0).astype(F32)
            grad = (acc[f, 0, here] + acc[f, 1, here]) * slope[4 * f + r]
            slope[4 * f + r] = grad
            one_sum = one_sum + grad * live
            two_sum = two_sum + grad * hat[4 * f + r] * live
    sums = fold_groups(jnp.sum(one_sum, axis=0, keepdims=True), jnp.sum(two_sum, axis=0, keepdims=True))
    ar_begin(1, 0, sums)
    stage_a_sent()
    for role, sent_by in ((0, (1, 2)), (1, (0, 3))):
        @pl.when(c == role)
        def _():
            for which in sent_by:
                small_copy(which).wait_send()
            shared = [n + str(k) for k in range(SHARED) for n in ("or", "ol", "zo")] if role == 0 else []
            tables[role].sent(*[n for n in tables[role].entries if n[0] != "a" and n not in shared])
            if role == 0:
                for k in range(SHARED):
                    mine_to_fetch(k, lambda k=k: tables[0].sent(f"or{k}", f"ol{k}", f"zo{k}"))
    for which in (4, 5):
        small_copy(which).wait_send()
    for step in range(2):
        for k in range((31, 15)[step]):
            ar_copy(0, step, k).wait_send()
    ar_begin(1, 1, ar_end(1, 0))
    for k in range(31):
        ar_copy(1, 0, k).wait_send()
    both = unfold_groups(ar_end(1, 1)) * (1.0 / COUNT)
    b_one, b_two = row_of(both, 0), row_of(both, 4)
    for f in range(3):
        for r in range(4):
            here = slice(16 * r, 16 * r + 16)
            live = jnp.where((f < fl) & (r < rl), 1.0, 0.0).astype(F32)
            value = rstd_row * (slope[4 * f + r] - (b_one + hat[4 * f + r] * b_two))
            out_ref[f, r] = (value + (skip[f, 0, here] + skip[f, 1, here])) * live
    for k in range(15):
        ar_copy(1, 1, k).wait_send()


def shards(coarse_input, cotangent, conv_kernel, short_kernel, norm_gain, norm_bias, frame_lengths, row_lengths):
    vmem = pl.BlockSpec(memory_space=pltpu.VMEM)
    anywhere = pl.BlockSpec(memory_space=pl.ANY)
    copies = (7 + 48 + SHARED + 14 + 32, 7 + 6 + 56 + 32)
    return pl.pallas_call(
        kernel,
        out_shape=jax.ShapeDtypeStruct((3, 4, 16, 512), F32),
        in_specs=[anywhere] * 8,
        out_specs=vmem,
        scratch_shapes=[
            pltpu.SMEM((64,), jnp.int32),
            pltpu.SMEM((8,), jnp.int32),
            pltpu.VMEM((3, 4, 16, 512), BF),
            pltpu.VMEM((3, 8, 32, 256), BF),
            pltpu.VMEM((1, 512), F32),
            pltpu.VMEM((1, 512), F32),
            pltpu.SemaphoreType.DMA((8,)),
            pltpu.VMEM((28, 4, 256, 128), BF),
            pltpu.VMEM((28, 4, 128), BF),
            pltpu.VMEM((8, 17, 4, 128), BF),
            pltpu.VMEM((17, 32, 128), F32),
            pltpu.VMEM((3, 8, 32, 256), BF),
            pltpu.VMEM((8, 32, 256), BF),
            pltpu.VMEM((2, 5, 32, 256), BF),
            pltpu.VMEM((2, 5, 32, 256), BF),
            pltpu.VMEM((5, 10, 32, 256), BF),
            pltpu.VMEM((576, 320), BF),
            pltpu.VMEM((5, 2, 9, 64, 256), BF),
            pltpu.VMEM((3, 2, 64, 512), F32),
            pltpu.VMEM((3, 2, 64, 512), F32),
            pltpu.VMEM((12, 16, 512), F32),
            pltpu.VMEM((12, 16, 512), F32),
            pltpu.VMEM((2, 32, 1, 128), F32),
            pltpu.VMEM((2, 16, 1, 128), F32),
            pltpu.SemaphoreType.DMA((2, 31)),
            pltpu.SemaphoreType.DMA((2, 31)),
            pltpu.SemaphoreType.DMA((2, 15)),
            pltpu.SemaphoreType.DMA((2, 15)),
            pltpu.SemaphoreType.DMA((6,)),
            pltpu.SemaphoreType.DMA((6,)),
            pltpu.SemaphoreType.DMA((copies[0],)),
            pltpu.SemaphoreType.DMA((copies[0],)),
            pltpu.SemaphoreType.DMA((copies[1],)),
            pltpu.SemaphoreType.DMA((copies[1],)),
        ],
        compiler_params=pltpu.CompilerParams(
            collective_id=0, has_side_effects=True, vmem_limit_bytes=60 * 1024 * 1024
        ),
    )(
        frame_lengths, row_lengths, coarse_input, cotangent,
        conv_kernel.transpose(0, 2, 1), short_kernel.transpose(0, 2, 1),
        norm_gain.reshape(1, 512), norm_bias.reshape(1, 512),
    )


def solution(mesh):
    return jax.shard_map(
        shards,
        mesh=mesh,
        in_specs=(
            P("tm", "height", None, None),
            P("tm", "height", None, None),
            P(None, None, "tm"),
            P(None, None, "tm"),
            P(),
            P(),
            P(),
            P(),
        ),
        out_specs=P("tm", "height", None, None),
        check_vma=False,
    )
```

```python
import functools

import jax
import jax.numpy as jnp
from jax import lax
from jax.experimental import pallas as pl
from jax.experimental.pallas import tpu as pltpu
from jax.sharding import PartitionSpec as P

EPSILON = 1e-06
COUNT = 422144.0
TAPS = ((0, 15), (15, 13))
SHARED = 6
BF = jnp.bfloat16
F32 = jnp.float32


def mod(value, n):
    return lax.rem(value + n, n)


class Table:
    def __init__(self, send, recv):
        self.send, self.recv, self.entries, self.count = send, recv, {}, 0

    def add(self, name, src, dst, device):
        self.entries[name] = (src, dst, device, self.count)
        self.count += 1

    def get(self, name):
        src, dst, device, at = self.entries[name]
        return pltpu.make_async_remote_copy(
            src_ref=src() if callable(src) else src,
            dst_ref=dst() if callable(dst) else dst,
            send_sem=self.send.at[at],
            recv_sem=self.recv.at[at],
            device_id=device,
            device_id_type=pl.DeviceIdType.MESH,
        )

    def start(self, *names):
        for name in names:
            self.get(name).start()

    def arrive(self, *names):
        for name in names:
            self.get(name).wait_recv()

    def sent(self, *names):
        for name in names:
            self.get(name).wait_send()


def ring_distance(d, n):
    return min(d, n - d)


PLANE = sorted(
    [(dx, dy) for dx in range(4) for dy in range(8) if dx + dy],
    key=lambda d: -(ring_distance(d[0], 4) + ring_distance(d[1], 8)),
)
COLUMN = sorted(
    [(dz, dc) for dz in range(8) for dc in range(2) if dz + dc],
    key=lambda d: -(ring_distance(d[0], 8) + d[1]),
)


def kernel(
    fl_any, rl_any, y_any, g_any, wc_any, ws_any, gain_any, bias_any, out_ref,
    fl_ref, rl_ref, y_ref, g_ref, gain_ref, bias_ref, load_sem,
    whole, mine, slots, rows32, ahead, chosen_next, edge_out, edge_in, padded, chosen, windows,
    acc, skip, hat, slope, plane, column, plane_send, plane_recv, column_send, column_recv,
    small_send, small_recv, send0, recv0, send1, recv1,
):
    tm, height = lax.axis_index("tm"), lax.axis_index("height")
    y, h, c = tm // 8, lax.rem(tm // 2, 4), lax.rem(tm, 2)
    x, zl = height // 2, lax.rem(height, 2)
    z = h * 2 + zl

    def at(y_=y, z_=z, c_=c, x_=x):
        return (y_ * 8 + (z_ // 2) * 2 + c_, x_ * 2 + lax.rem(z_, 2))

    def plane_device(d):
        return at(x_=lax.rem(x + d[0], 4), y_=lax.rem(y + d[1], 8))

    def column_device(d):
        return at(z_=lax.rem(z + d[0], 8), c_=lax.rem(c + d[1], 2))

    partners = [plane_device(d) for d in PLANE] + [column_device(d) for d in COLUMN]
    for d in (1, 2, 62, 63):
        partners.append((lax.rem(tm + d, 64), height))
    for d in (1, 7):
        partners.append((tm, lax.rem(height + d, 8)))
    barrier = pltpu.get_barrier_semaphore()
    for partner in partners:
        pl.semaphore_signal(barrier, inc=1, device_id=partner, device_id_type=pl.DeviceIdType.MESH)
    lanes = pl.ds(pl.multiple_of(x * 128, 128), 128)
    loads = [
        pltpu.make_async_copy(src, dst, load_sem.at[k])
        for k, (src, dst) in enumerate((
            (wc_any.at[:, :, lanes], mine.at[pl.ds(0, 27)]), (ws_any.at[:, :, lanes], mine.at[pl.ds(27, 1)]),
            (g_any, g_ref), (fl_any, fl_ref),
            (rl_any, rl_ref), (y_any, y_ref), (gain_any, gain_ref), (bias_any, bias_ref),
        ))
    ]
    for load in loads:
        load.start()

    def ar_copy(turn, step, k):
        if step == 0:
            place, device = plane.at[turn, x * 8 + y], plane_device(PLANE[k])
            sems = plane_send.at[turn, k], plane_recv.at[turn, k]
        else:
            place, device = column.at[turn, z * 2 + c], column_device(COLUMN[k])
            sems = column_send.at[turn, k], column_recv.at[turn, k]
        return pltpu.make_async_remote_copy(
            src_ref=place, dst_ref=place, send_sem=sems[0], recv_sem=sems[1],
            device_id=device, device_id_type=pl.DeviceIdType.MESH,
        )

    def ar_begin(turn, step, value):
        if step == 0:
            plane[turn, x * 8 + y] = value
        else:
            column[turn, z * 2 + c] = value
        for k in range((31, 15)[step]):
            ar_copy(turn, step, k).start()

    def ar_end(turn, step):
        for k in range((31, 15)[step]):
            ar_copy(turn, step, k).wait_recv()
        return jnp.sum((plane, column)[step][turn], axis=0)

    def row_of(tile, base):
        return jnp.concatenate([tile[base + k : base + k + 1] for k in range(4)], axis=1)

    lane_i = lax.broadcasted_iota(jnp.int32, (128, 128), 0)
    lane_j = lax.broadcasted_iota(jnp.int32, (128, 128), 1)
    fold = jnp.where((lane_i >> 4) == (lane_j & 7), 1.0, 0.0).astype(F32)
    unfold = jnp.where((lane_i & 7) == (lane_j >> 4), 1.0, 0.0).astype(F32)
    own_lanes = lax.broadcasted_iota(jnp.int32, (8, 128), 0) == (
        lax.broadcasted_iota(jnp.int32, (8, 128), 1) >> 3
    )

    def fold_groups(first, second):
        parts = [v[:, 128 * k : 128 * k + 128] for v in (first, second) for k in range(4)]
        tile = jnp.concatenate(parts, axis=0)
        sums = jnp.dot(tile, fold, precision=lax.Precision.HIGHEST, preferred_element_type=F32)
        return jnp.sum(jnp.where(own_lanes, sums, 0.0), axis=0, keepdims=True)

    def unfold_groups(row):
        tile = jnp.where(own_lanes, jnp.broadcast_to(row, (8, 128)), 0.0)
        return jnp.dot(tile, unfold, precision=lax.Precision.HIGHEST, preferred_element_type=F32)

    def table(role):
        t0, taps = TAPS[role]
        half = taps // 2
        t = Table(send0 if role == 0 else send1, recv0 if role == 0 else recv1)

        def piece(column, block, lo=0, n=taps):
            row = pl.multiple_of(block * 32, 32)
            return whole.at[pl.ds(t0 + lo, n), column, pl.ds(row, 32)]

        src = mine.at[pl.ds(t0, taps)]
        place = slots.at[h * 2 + c, pl.ds(0, taps)]
        for d in range(1, 4):
            device = at(z_=mod(z + (2 * zl - 1) * d, 8), c_=role)
            t.add(f"a{d}0", src, place, device)
            t.add(f"a{d}1", src, place, device)
        t.add("as", src, place, at(c_=role))
        columns = [x, mod(x - 1, 4), mod(x + 1, 4), mod(x + 2, 4)]
        blocks = [y]
        for s in range(1, 4):
            blocks += [mod(y - s, 8), mod(y + s, 8)]
        blocks.append(mod(y + 4, 8))
        left, right = at(x_=mod(x - 1, 4)), at(x_=mod(x + 1, 4))
        up, down = at(y_=mod(y + 1, 8)), at(y_=mod(y - 1, 8))
        parts = ((0, half), (half, taps - half))
        for k in range(8 if role == 0 else 1):
            for q in (0, 1):
                ref = piece(columns[0], blocks[k], *parts[q])
                t.add(f"xr{k}{q}", ref, ref, right)
                t.add(f"xl{k}{q}", ref, ref, left)
            ref = piece(columns[1], blocks[k], *parts[0])
            t.add(f"or{k}", ref, ref, right)
            ref = piece(columns[2], blocks[k], *parts[1])
            t.add(f"ol{k}", ref, ref, left)
            if role == 0 and k < SHARED:
                ref = piece(columns[3], blocks[k])
                t.add(f"zo{k}", ref, ref, at(z_=z + 1 - 2 * zl))
        for j in range(1 if role == 0 else 4):
            for s in range(4):
                for q in (0, 1):
                    if s < 3 or q == 0:
                        ref = piece(columns[j], mod(y - s, 8), *parts[q])
                        t.add(f"yp{j}{s}{q}", ref, ref, up)
                    if s < 3 or q == 1:
                        ref = piece(columns[j], mod(y + s, 8), *parts[q])
                        t.add(f"ym{j}{s}{q}", ref, ref, down)
        for k in range(8):
            for j in range(4):
                ref = piece(columns[j], blocks[k])
                t.add(f"d{k}{j}", ref, ref, at(c_=1 - role))
        return t

    tables = (table(0), table(1))

    def stage_a_send():
        for role in (0, 1):
            @pl.when(c == 0)
            def _():
                for d in range(1, 4):
                    tables[role].start(f"a{d}0")

            @pl.when(c == 1)
            def _():
                for d in range(1, 4):
                    tables[role].start(f"a{d}1")

            @pl.when(c == 1 - role)
            def _():
                tables[role].start("as")

    def stage_a_sent():
        for role in (0, 1):
            @pl.when(c == 0)
            def _():
                for d in range(1, 4):
                    tables[role].sent(f"a{d}0")

            @pl.when(c == 1)
            def _():
                for d in range(1, 4):
                    tables[role].sent(f"a{d}1")

            @pl.when(c == 1 - role)
            def _():
                tables[role].sent("as")

    def stage_a_arrive(role):
        t0, taps = TAPS[role]
        t = tables[role]
        slots[h * 2 + role, 0:taps] = mine[t0 : t0 + taps]
        for d in range(1, 4):
            t.arrive(f"a{d}0", f"a{d}1")
        t.arrive("as")
        row = pl.multiple_of(y * 32, 32)
        for s in range(8):
            rows32[0:taps, 4 * s : 4 * s + 4] = slots[s, 0:taps].astype(F32)
        whole[t0 : t0 + taps, x, pl.ds(row, 32)] = rows32[0:taps].astype(BF)

    def begin(role):
        t = tables[role]
        for q in (0, 1):
            both = [f"yp00{q}", f"ym00{q}", f"xr0{q}", f"xl0{q}"]
            t.start(*(both if role == 0 else both[2:] + both[:2]))
        t.start("d00")

    def mine_to_fetch(k, act, otherwise=None):
        if k >= SHARED:
            act()
            return
        pl.when(zl == k % 2)(act)
        if otherwise is not None:
            pl.when(zl != k % 2)(otherwise)

    def x_in0(k):
        t = tables[0]
        t.arrive(f"xr{k}0")
        mine_to_fetch(k, lambda: t.start(f"or{k}"))
        t.arrive(f"xl{k}1")
        mine_to_fetch(k, lambda: t.start(f"ol{k}"))
        t.arrive(f"xr{k}1")
        t.start(f"d{k}1")
        t.arrive(f"xl{k}0")
        t.start(f"d{k}2")

    def o_in0(k):
        t = tables[0]

        def fetched():
            t.arrive(f"or{k}", f"ol{k}")
            if k < SHARED:
                t.start(f"zo{k}")
            t.start(f"d{k}3")

        def given():
            t.arrive(f"zo{k - 2}")
            t.start(f"d{k - 2}3")

        mine_to_fetch(k, fetched)
        if 0 <= k - 2 < SHARED:
            pl.when(zl != k % 2)(given)

    def y_in0(s):
        t = tables[0]
        k = 2 * s - 1
        for q in (0, 1):
            if s < 4 or q == 0:
                t.arrive(f"yp0{s - 1}{q}")
                if s < 3 or (s == 3 and q == 0):
                    t.start(f"yp0{s}{q}")
                t.start(f"xr{k}{q}", f"xl{k}{q}")
            if s < 4 or q == 1:
                t.arrive(f"ym0{s - 1}{q}")
                if s < 3 or (s == 3 and q == 1):
                    t.start(f"ym0{s}{q}")
                m = min(k + 1, 7)
                t.start(f"xr{m}{q}", f"xl{m}{q}")
        t.start(f"d{k}0")
        if s < 4:
            t.start(f"d{k + 1}0")

    def x_in1():
        t = tables[1]
        for q in (0, 1):
            t.arrive(f"xr0{q}")
            t.start(f"yp10{q}", f"ym10{q}")
            if q == 0:
                t.start("or0")
        for q in (1, 0):
            t.arrive(f"xl0{q}")
            if q == 1:
                t.start("ol0")
            t.start(f"yp20{q}", f"ym20{q}")
        t.start("d01", "d02")

    def o_in1():
        t = tables[1]
        t.arrive("or0")
        t.start("yp300", "ym300")
        t.arrive("ol0")
        t.start("yp301", "ym301", "d03")

    def y_in1(s, chains=(0, 1, 2, 3)):
        t = tables[1]
        for j in chains:
            for q in (0, 1):
                if s < 4 or q == 0:
                    t.arrive(f"yp{j}{s - 1}{q}")
                    if s < 3 or (s == 3 and q == 0):
                        t.start(f"yp{j}{s}{q}")
                if s < 4 or q == 1:
                    t.arrive(f"ym{j}{s - 1}{q}")
                    if s < 3 or (s == 3 and q == 1):
                        t.start(f"ym{j}{s}{q}")
            t.start(f"d{2 * s - 1}{j}")
            if s < 4:
                t.start(f"d{2 * s}{j}")

    def small_copy(which):
        before, sibling = (mod(tm - 1, 64), height), at(c_=1 - c)
        if which == 0:
            src, dst, device = g_ref.at[pl.ds(0, 2)], ahead.at[pl.ds(0, 2)], sibling
        elif which == 1:
            src, dst, device = g_ref.at[0], ahead.at[0], before
        elif which == 2:
            src, dst, device = chosen_next, ahead.at[1], before
        elif which == 3:
            src, dst, device = ahead.at[0], ahead.at[2], sibling
        elif which == 4:
            src, dst, device = edge_out.at[1], edge_in.at[0], (tm, mod(height + 1, 8))
        else:
            src, dst, device = edge_out.at[0], edge_in.at[1], (tm, mod(height - 1, 8))
        return pltpu.make_async_remote_copy(
            src_ref=src, dst_ref=dst, send_sem=small_send.at[which], recv_sem=small_recv.at[which],
            device_id=device, device_id_type=pl.DeviceIdType.MESH,
        )

    zero_frame = jnp.zeros((8, 32, 256), BF)
    zero_row = jnp.zeros((32, 256), BF)

    def frames_begin():
        @pl.when(c == 0)
        def _():
            small_copy(1).start()

        @pl.when(c == 1)
        def _():
            small_copy(0).start()

    def frames_choose():
        @pl.when(c == 0)
        def _():
            small_copy(0).wait_recv()
            chosen_next[...] = lax.select(fl >= 2, g_ref[1], ahead[0])
            small_copy(2).start()

    def frames_pass():
        @pl.when(c == 1)
        def _():
            small_copy(1).wait_recv()
            small_copy(3).start()

    def order_frames():
        @pl.when(c == 0)
        def _():
            small_copy(3).wait_recv()

        @pl.when(c == 1)
        def _():
            small_copy(2).wait_recv()

        has_one = tm < 63
        has_two = jnp.logical_and(has_one, jnp.logical_or(fl_next >= 2, tm < 62))
        following = lax.select(has_one, ahead[0], zero_frame)
        after = lax.select(jnp.logical_or(c == 1, fl_next >= 2), ahead[1], ahead[2])
        after = lax.select(has_two, after, zero_frame)
        own = [g_ref[0], g_ref[1], g_ref[2]]
        ordered = [
            own[0],
            lax.select(fl >= 2, own[1], following),
            lax.select(fl >= 3, own[2], lax.select(fl == 2, following, after)),
            lax.select(fl >= 3, following, lax.select(fl == 2, after, zero_frame)),
            lax.select(fl >= 3, after, zero_frame),
        ]
        for p in range(5):
            last = ordered[p][1]
            for r in range(8):
                row = ordered[p][r]
                if r >= 2:
                    row = lax.select(r < 2 * rl, row, zero_row)
                if r >= 3 and r % 2 == 1:
                    last = lax.select(r == 2 * rl - 1, row, last)
                padded[p, r + 1] = row
            edge_out[0, p] = ordered[p][0]
            edge_out[1, p] = last
        small_copy(4).start()
        small_copy(5).start()

    def finish_rows():
        small_copy(4).wait_recv()
        small_copy(5).wait_recv()
        for p in range(5):
            above = lax.select(height > 0, edge_in[0, p], zero_row)
            below = lax.select(height < 7, edge_in[1, p], zero_row)
            padded[p, 0] = above
            for r in (2, 4, 6):
                padded[p, r + 1] = lax.select(r == 2 * rl, below, padded[p, r + 1])
            padded[p, 9] = lax.select(rl == 4, below, zero_row)

    def make_chosen():
        out_row = lax.broadcasted_iota(jnp.int32, (64, 320), 0)
        in_row = lax.broadcasted_iota(jnp.int32, (64, 320), 1)
        down_by = (in_row >> 5) - 2 * (out_row >> 4)
        along_by = (in_row & 31) - 2 * (out_row & 15)
        choose = []
        for kh in range(3):
            for kw in range(3):
                dr, dc = down_by - (2 - kh), along_by - (1 - kw)
                hit = ((dr == 0) | (dr == 1)) & ((dc == 0) | (dc == 1))
                choose.append(jnp.where(hit, 1.0, 0.0).astype(F32))
        chosen[...] = jnp.concatenate(choose, axis=0).astype(BF)

    def make_windows(*frames):
        for f in frames:
            total = jnp.dot(chosen[...], padded[f].reshape(320, 256), preferred_element_type=F32)
            top = total.astype(BF)
            rest = (total - top.astype(F32)).astype(BF)
            windows[f, 0] = top.reshape(9, 64, 256)
            windows[f, 1] = rest.reshape(9, 64, 256)

    def statistics(total):
        gs = unfold_groups(total) * (1.0 / COUNT)
        mean, msq = gs[0:4], gs[4:8]
        rstd = lax.rsqrt(msq - mean * mean + EPSILON)
        mean_row, rstd_row = row_of(mean, 0), row_of(rstd, 0)
        return mean_row, rstd_row

    def make_slope(low, high, mean_row, rstd_row):
        gain, bias = gain_ref[...], bias_ref[...]

        def one(i, carry):
            value = (y_ref[i // 4, lax.rem(i, 4)].astype(F32) - mean_row) * rstd_row
            pre = value * gain + bias
            sig = jax.nn.sigmoid(pre)
            hat[i] = value
            slope[i] = sig * (1.0 + pre * (1.0 - sig)) * gain
            return carry

        lax.fori_loop(low, high, one, 0)

    loads[0].wait()
    loads[1].wait()
    pl.semaphore_wait(barrier, len(partners))
    stage_a_send()
    for load in loads[2:]:
        load.wait()
    fl, rl = fl_ref[tm], rl_ref[height]
    fl_next = fl_ref[mod(tm + 1, 64)]

    first = jnp.zeros((16, 512), F32)
    second = jnp.zeros((16, 512), F32)
    for f in range(3):
        for r in range(4):
            live = jnp.where((f < fl) & (r < rl), 1.0, 0.0).astype(F32)
            value = y_ref[f, r].astype(F32) * live
            first = first + value
            second = second + value * value
    stats = fold_groups(jnp.sum(first, axis=0, keepdims=True), jnp.sum(second, axis=0, keepdims=True))
    ar_begin(0, 0, stats)
    make_chosen()

    @pl.when(c == 0)
    def _():
        stage_a_arrive(0)
        begin(0)

    @pl.when(c == 1)
    def _():
        stage_a_arrive(1)
        begin(1)

    frames_begin()
    ar_begin(0, 1, ar_end(0, 0))
    frames_choose()

    @pl.when(c == 0)
    def _():
        y_in0(1)
        x_in0(0)

    @pl.when(c == 1)
    def _():
        x_in1()
        y_in1(1, (0,))
        o_in1()

    frames_pass()

    @pl.when(c == 0)
    def _():
        y_in0(2)
        x_in0(1)
        o_in0(0)
        x_in0(2)

    @pl.when(c == 1)
    def _():
        y_in1(1, (1, 2, 3))

    @pl.when(c == 0)
    def _():
        y_in0(3)
        o_in0(1)
        x_in0(3)

    @pl.when(c == 1)
    def _():
        y_in1(2, (0, 1))

    order_frames()

    @pl.when(c == 0)
    def _():
        o_in0(2)
        x_in0(4)
        y_in0(4)

    @pl.when(c == 1)
    def _():
        y_in1(2, (2, 3))

    mean_row, rstd_row = statistics(ar_end(0, 1))
    make_slope(0, 6, mean_row, rstd_row)

    @pl.when(c == 0)
    def _():
        o_in0(3)
        x_in0(5)

    @pl.when(c == 1)
    def _():
        y_in1(3, (0, 1))

    finish_rows()
    make_windows(0, 1)

    @pl.when(c == 0)
    def _():
        o_in0(4)
        x_in0(6)

    @pl.when(c == 1)
    def _():
        y_in1(3, (2, 3))

    make_windows(2, 3)

    @pl.when(c == 0)
    def _():
        o_in0(5)
        x_in0(7)

    @pl.when(c == 1)
    def _():
        y_in1(4, (0, 1))

    make_windows(4)
    make_slope(6, 12, mean_row, rstd_row)

    @pl.when(c == 0)
    def _():
        o_in0(6)
        for k in range(8):
            tables[1].arrive(*[f"d{k}{j}" for j in range(4)])

    @pl.when(c == 1)
    def _():
        y_in1(4, (2, 3))

    def kernel_rows(first_tap, n):
        block = whole[pl.ds(first_tap, n)]
        return jnp.concatenate([block[:, k].reshape(n * 256, 128) for k in range(4)], axis=1)

    def taps_of(i, carry):
        kt, kh = i // 3, lax.rem(i, 3)
        lhs = jnp.concatenate(
            [windows[pl.ds(2 - kt, 3), :, kh * 3 + kw].reshape(384, 256) for kw in range(3)], axis=1
        )
        acc[...] += jnp.dot(lhs, kernel_rows(3 * i, 3), preferred_element_type=F32).reshape(3, 2, 64, 512)
        return carry

    skip[...] = jnp.dot(
        windows[0:3, :, 4].reshape(384, 256), kernel_rows(27, 1), preferred_element_type=F32
    ).reshape(3, 2, 64, 512)
    acc[...] = jnp.zeros_like(acc)
    lax.fori_loop(6, 9, taps_of, 0)

    @pl.when(c == 0)
    def _():
        o_in0(7)

    @pl.when(c == 1)
    def _():
        for k in range(8):
            tables[0].arrive(*[f"d{k}{j}" for j in range(4)])

    lax.fori_loop(0, 6, taps_of, 0)

    one_sum = jnp.zeros((16, 512), F32)
    two_sum = jnp.zeros((16, 512), F32)
    for f in range(3):
        for r in range(4):
            here = slice(16 * r, 16 * r + 16)
            live = jnp.where((f < fl) & (r < rl), 1.0, 0.0).astype(F32)
            grad = (acc[f, 0, here] + acc[f, 1, here]) * slope[4 * f + r]
            slope[4 * f + r] = grad
            one_sum = one_sum + grad * live
            two_sum = two_sum + grad * hat[4 * f + r] * live
    sums = fold_groups(jnp.sum(one_sum, axis=0, keepdims=True), jnp.sum(two_sum, axis=0, keepdims=True))
    ar_begin(1, 0, sums)
    stage_a_sent()
    for role, sent_by in ((0, (1, 2)), (1, (0, 3))):
        @pl.when(c == role)
        def _():
            for which in sent_by:
                small_copy(which).wait_send()
            shared = [n + str(k) for k in range(SHARED) for n in ("or", "ol", "zo")] if role == 0 else []
            tables[role].sent(*[n for n in tables[role].entries if n[0] != "a" and n not in shared])
            if role == 0:
                for k in range(SHARED):
                    mine_to_fetch(k, lambda k=k: tables[0].sent(f"or{k}", f"ol{k}", f"zo{k}"))
    for which in (4, 5):
        small_copy(which).wait_send()
    for step in range(2):
        for k in range((31, 15)[step]):
            ar_copy(0, step, k).wait_send()
    ar_begin(1, 1, ar_end(1, 0))
    for k in range(31):
        ar_copy(1, 0, k).wait_send()
    both = unfold_groups(ar_end(1, 1)) * (1.0 / COUNT)
    b_one, b_two = row_of(both, 0), row_of(both, 4)
    for f in range(3):
        for r in range(4):
            here = slice(16 * r, 16 * r + 16)
            live = jnp.where((f < fl) & (r < rl), 1.0, 0.0).astype(F32)
            value = rstd_row * (slope[4 * f + r] - (b_one + hat[4 * f + r] * b_two))
            out_ref[f, r] = (value + (skip[f, 0, here] + skip[f, 1, here])) * live
    for k in range(15):
        ar_copy(1, 1, k).wait_send()


def shards(coarse_input, cotangent, conv_kernel, short_kernel, norm_gain, norm_bias, frame_lengths, row_lengths):
    vmem = pl.BlockSpec(memory_space=pltpu.VMEM)
    anywhere = pl.BlockSpec(memory_space=pl.ANY)
    copies = (7 + 48 + SHARED + 14 + 32, 7 + 6 + 56 + 32)
    return pl.pallas_call(
        kernel,
        out_shape=jax.ShapeDtypeStruct((3, 4, 16, 512), F32),
        in_specs=[anywhere] * 8,
        out_specs=vmem,
        scratch_shapes=[
            pltpu.SMEM((64,), jnp.int32),
            pltpu.SMEM((8,), jnp.int32),
            pltpu.VMEM((3, 4, 16, 512), BF),
            pltpu.VMEM((3, 8, 32, 256), BF),
            pltpu.VMEM((1, 512), F32),
            pltpu.VMEM((1, 512), F32),
            pltpu.SemaphoreType.DMA((8,)),
            pltpu.VMEM((28, 4, 256, 128), BF),
            pltpu.VMEM((28, 4, 128), BF),
            pltpu.VMEM((8, 17, 4, 128), BF),
            pltpu.VMEM((17, 32, 128), F32),
            pltpu.VMEM((3, 8, 32, 256), BF),
            pltpu.VMEM((8, 32, 256), BF),
            pltpu.VMEM((2, 5, 32, 256), BF),
            pltpu.VMEM((2, 5, 32, 256), BF),
            pltpu.VMEM((5, 10, 32, 256), BF),
            pltpu.VMEM((576, 320), BF),
            pltpu.VMEM((5, 2, 9, 64, 256), BF),
            pltpu.VMEM((3, 2, 64, 512), F32),
            pltpu.VMEM((3, 2, 64, 512), F32),
            pltpu.VMEM((12, 16, 512), F32),
            pltpu.VMEM((12, 16, 512), F32),
            pltpu.VMEM((2, 32, 1, 128), F32),
            pltpu.VMEM((2, 16, 1, 128), F32),
            pltpu.SemaphoreType.DMA((2, 31)),
            pltpu.SemaphoreType.DMA((2, 31)),
            pltpu.SemaphoreType.DMA((2, 15)),
            pltpu.SemaphoreType.DMA((2, 15)),
            pltpu.SemaphoreType.DMA((6,)),
            pltpu.SemaphoreType.DMA((6,)),
            pltpu.SemaphoreType.DMA((copies[0],)),
            pltpu.SemaphoreType.DMA((copies[0],)),
            pltpu.SemaphoreType.DMA((copies[1],)),
            pltpu.SemaphoreType.DMA((copies[1],)),
        ],
        compiler_params=pltpu.CompilerParams(
            collective_id=0, has_side_effects=True, vmem_limit_bytes=60 * 1024 * 1024
        ),
    )(
        frame_lengths, row_lengths, coarse_input, cotangent,
        conv_kernel.transpose(0, 2, 1), short_kernel.transpose(0, 2, 1),
        norm_gain.reshape(1, 512), norm_bias.reshape(1, 512),
    )


def solution(mesh):
    return jax.shard_map(
        shards,
        mesh=mesh,
        in_specs=(
            P("tm", "height", None, None),
            P("tm", "height", None, None),
            P(None, None, "tm"),
            P(None, None, "tm"),
            P(),
            P(),
            P(),
            P(),
        ),
        out_specs=P("tm", "height", None, None),
        check_vma=False,
    )
```
